256 devices in a mesh: band: 8 (over z), tile: 32 (over x, y, core).
Axes of the slice: x: 4, y: 4, z: 8, core: 2. Of those that a mesh axis runs over, the one named last changes fastest.
Arguments:
- queries: bfloat16 [2048, 512], replicated, may hold values from -15 to 15
- query_pos: bfloat16 [2048, 512], replicated, may hold values from -6 to 6
- patches: bfloat16 [131072, 512], P(('band', 'tile')), may hold values from -6 to 6
- patch_level: int32 [131072], P(('band', 'tile')), may hold values from 0 to 3
- patch_sheet: int32 [131072], P(('band', 'tile')), may hold values from 0 to 15, as said below
- query_sheets: int32 [2048, 16], replicated, may hold values from 0 to 1, as said below
- level_embed: bfloat16 [4, 512], replicated, may hold values from -6 to 6
- cross_proj: bfloat16 [4, 512, 512], replicated, may hold values from -0.25 to 0.25
- self_proj: bfloat16 [4, 512, 512], replicated, may hold values from -0.25 to 0.25
- mlp_in: bfloat16 [512, 2048], replicated, may hold values from -0.25 to 0.25
- mlp_out: bfloat16 [2048, 512], replicated, may hold values from -0.125 to 0.125
- norm_gain: float32 [3, 512], replicated, may hold values from 0.5 to 1.5
Outputs:
- decoded: bfloat16 [2048, 512], P('tile')
The draws below stay inside these ranges and needn't reach their ends.
Inputs may be any that keep to these rules, and one draw needn't show every extreme that they name: `patch_sheet`: the patches of rows b * 16384 to (b + 1) * 16384 - 1 lie on sheets b * 2 to (b + 1) * 2 - 1, and each of these sheets holds one or more of them. `query_sheets`: every query may look at one sheet or more.
All inputs are finite; a program needn't handle non-finite values.
Results may differ from the reference program's by a relative error of at most 0.025.
Values may be sent and summed in bfloat16 or wider, within the bound.
No kernel may reach another device: no remote copies, remote signals or barrier semaphores. Data moves between devices by JAX's collectives and lax.ppermute only.
A program may use at most 192 MiB of HBM per device.

```python
import math
import jax
import jax.numpy as jnp
from jax import lax

D = 512
HEADS = 8
FF = 2048
Q = 2048
LEVELS = 4
SHEETS = 16
PATCHES = 131072
BAND_ROWS = 16384
SHEETS_BAND = 2


def draw_queries(key, part):
    key = jax.random.fold_in(key, 11)
    base_key = jax.random.fold_in(key, 0)
    values = jax.random.normal(base_key, (Q, D), jnp.float32) * 3.0
    return jnp.clip(values, -15.0, 15.0).astype(jnp.bfloat16)


def draw_patch_sheet(key, part):
    key = jax.random.fold_in(key, 23)
    rows = jnp.arange(PATCHES, dtype=jnp.int32)
    inside = rows % BAND_ROWS
    picked = jax.random.randint(key, (PATCHES,), 0, SHEETS_BAND, dtype=jnp.int32)
    offset = jnp.where(inside < SHEETS_BAND, inside, picked)
    return (rows // BAND_ROWS * SHEETS_BAND + offset).astype(jnp.int32)


def draw_query_sheets(key, part):
    key = jax.random.fold_in(key, 37)
    coin_key, force_key = jax.random.split(key)
    coins = jax.random.randint(coin_key, (Q, SHEETS), 0, 2, dtype=jnp.int32)
    forced = jax.random.randint(force_key, (Q,), 0, SHEETS, dtype=jnp.int32)
    chosen = (forced[:, None] == jnp.arange(SHEETS, dtype=jnp.int32)[None, :]).astype(jnp.int32)
    return jnp.maximum(coins, chosen).astype(jnp.int32)


def plant(array, own_key, smallest, high):
    place = [jax.random.randint(jax.random.fold_in(own_key, axis), (), 0, length) for axis, length in enumerate(array.shape)]
    widest = array.shape.index(max(array.shape))
    beside = place[:widest] + [(place[widest] + 1) % array.shape[widest]] + place[widest + 1:]
    return array.at[tuple(place)].set(smallest).at[tuple(beside)].set(high)


def level_of(key, extent, pieces, smallest, top_value):
    def one(position, shards_of):
        draws = jax.random.uniform(jax.random.fold_in(jax.random.fold_in(key, 6), position), (shards_of,), jnp.float32, smallest / len(pieces), top_value / len(pieces))
        return jnp.repeat(jnp.exp(draws), extent[position] // shards_of).reshape((-1,) + (1,) * (len(extent) - position - 1))

    factor_of = one(*pieces[0])
    for cut in pieces[1:]:
        factor_of = factor_of * one(*cut)
    return factor_of


def noise(rng, shape, width, limit, pieces=(), held_as=jnp.bfloat16):
    level = level_of(rng, shape, pieces, -0.22, 0.18) if pieces else 1.0
    values = jax.random.normal(rng, shape, jnp.float32) * width * level
    return jnp.minimum(jnp.maximum(values, -limit), limit).astype(held_as)


def setup_inputs(seed: int = 0) -> dict:
    arg_keys = jax.random.split(jax.random.key(seed), 13)
    return {
        "queries": draw_queries(jax.random.fold_in(arg_keys[12], 71), 0),
        "query_pos": noise(arg_keys[1], (Q, D), 1.0, 6.0),
        "patches": noise(arg_keys[2], (PATCHES, D), 1.0, 6.0, ((0, 256),)),
        "patch_level": plant(jax.random.randint(arg_keys[3], (PATCHES,), 0, LEVELS), jax.random.fold_in(arg_keys[3], 1), 0, LEVELS - 1).astype(jnp.int32),
        "patch_sheet": draw_patch_sheet(jax.random.fold_in(arg_keys[12], 71), 0),
        "query_sheets": draw_query_sheets(jax.random.fold_in(arg_keys[12], 71), 0),
        "level_embed": noise(arg_keys[6], (LEVELS, D), 1.0, 6.0),
        "cross_proj": noise(arg_keys[7], (4, D, D), D ** -0.5, 0.25),
        "self_proj": noise(arg_keys[8], (4, D, D), D ** -0.5, 0.25),
        "mlp_in": noise(arg_keys[9], (D, FF), D ** -0.5, 0.25),
        "mlp_out": noise(arg_keys[10], (FF, D), FF ** -0.5, 0.125),
        "norm_gain": jnp.clip(1.0 + 0.1 * jax.random.normal(arg_keys[11], (3, D), jnp.float32), 0.5, 1.5),
    }


def layer_norm(values, gain):
    center = lax.optimization_barrier(jnp.mean(values, axis=-1, keepdims=True))
    shifted = values - center
    spread = lax.optimization_barrier(jnp.mean(shifted * shifted, axis=-1, keepdims=True))
    return shifted * lax.rsqrt(spread + 1e-05) * gain

def self_attend(q_self, k_self, v_self, head_size):
    rows = q_self.shape[0]
    keys = k_self.shape[0]
    q_heads = q_self.astype(jnp.float32).reshape(rows, -1, head_size)
    k_heads = k_self.astype(jnp.float32).reshape(keys, -1, head_size)
    v_heads = v_self.astype(jnp.float32).reshape(keys, -1, head_size)
    scores = jnp.einsum('qhe,khe->hqk', q_heads, k_heads)
    peak = lax.optimization_barrier(jnp.max(scores, axis=-1, keepdims=True))
    weights = jnp.exp(scores - peak)
    probs = (weights / lax.optimization_barrier(jnp.sum(weights, axis=-1, keepdims=True))).astype(jnp.bfloat16).astype(jnp.float32)
    result = jnp.einsum('hqk,khe->qhe', probs, v_heads)
    return result.reshape(rows, -1).astype(jnp.bfloat16)

def reference(queries, query_pos, patches, patch_level, patch_sheet, query_sheets, level_embed, cross_proj, self_proj, mlp_in, mlp_out, norm_gain):
    head_size = D // HEADS
    score_scale = 1.0 / math.sqrt(head_size)
    mixed_in = queries + query_pos
    q_cross = (jnp.dot(mixed_in, cross_proj[0], preferred_element_type=jnp.float32) * score_scale).astype(jnp.bfloat16)
    level_rows = (patch_level[:, None] == jnp.arange(LEVELS, dtype=jnp.int32)[None, :]).astype(jnp.bfloat16)
    key_input = (patches.astype(jnp.float32) + jnp.dot(level_rows, level_embed, preferred_element_type=jnp.float32)).astype(jnp.bfloat16)
    k_cross = jnp.dot(key_input, cross_proj[1], preferred_element_type=jnp.float32).astype(jnp.bfloat16)
    v_cross = jnp.dot(patches, cross_proj[2], preferred_element_type=jnp.float32).astype(jnp.bfloat16)
    q_heads = q_cross.astype(jnp.float32).reshape(Q, HEADS, head_size)
    block = min(4096, PATCHES)
    count = PATCHES // block

    def block_scores(index):
        start = (index * block).astype(jnp.int32)
        keys = lax.dynamic_slice_in_dim(k_cross, start, block, 0).astype(jnp.float32).reshape(block, HEADS, head_size)
        sheets = lax.dynamic_slice_in_dim(patch_sheet, start, block, 0)
        scores = jnp.einsum('qhe,phe->hqp', q_heads, keys)
        allowed = jnp.take(query_sheets, sheets, axis=1) == 1
        return (scores, allowed, start)

    def peak_step(index, peak):
        scores, allowed, start = block_scores(index)
        masked = jnp.where(allowed[None], scores, -1e+30)
        return jnp.maximum(peak, lax.optimization_barrier(jnp.max(masked, axis=-1)))
    peak = lax.fori_loop(0, count, peak_step, jnp.full((HEADS, Q), -1e+30, jnp.float32))

    def sum_step(index, carry):
        numer, denom = carry
        scores, allowed, start = block_scores(index)
        weights = jnp.where(allowed[None], jnp.exp(scores - peak[:, :, None]), 0.0)
        values = lax.dynamic_slice_in_dim(v_cross, start, block, 0).astype(jnp.float32).reshape(block, HEADS, head_size)
        rounded = weights.astype(jnp.bfloat16).astype(jnp.float32)
        return (numer + jnp.einsum('hqp,phe->qhe', rounded, values), denom + lax.optimization_barrier(jnp.sum(weights, axis=-1)))
    numer, denom = lax.fori_loop(0, count, sum_step, (jnp.zeros((Q, HEADS, head_size), jnp.float32), jnp.zeros((HEADS, Q), jnp.float32)))
    attended = (numer / denom.T[:, :, None]).reshape(Q, D).astype(jnp.bfloat16)
    cross_out = jnp.dot(attended, cross_proj[3], preferred_element_type=jnp.float32)
    first_state = layer_norm(queries.astype(jnp.float32) + cross_out, norm_gain[0]).astype(jnp.bfloat16)
    self_in = first_state + query_pos
    q_self = (jnp.dot(self_in, self_proj[0], preferred_element_type=jnp.float32) * score_scale).astype(jnp.bfloat16)
    k_self = jnp.dot(self_in, self_proj[1], preferred_element_type=jnp.float32).astype(jnp.bfloat16)
    v_self = jnp.dot(first_state, self_proj[2], preferred_element_type=jnp.float32).astype(jnp.bfloat16)
    self_out = self_attend(q_self, k_self, v_self, head_size)
    second_state = layer_norm(first_state.astype(jnp.float32) + jnp.dot(self_out, self_proj[3], preferred_element_type=jnp.float32), norm_gain[1]).astype(jnp.bfloat16)
    hidden = jnp.maximum(jnp.dot(second_state, mlp_in, preferred_element_type=jnp.float32), 0.0).astype(jnp.bfloat16)
    return layer_norm(second_state.astype(jnp.float32) + jnp.dot(hidden, mlp_out, preferred_element_type=jnp.float32), norm_gain[2]).astype(jnp.bfloat16)
```

```python
import functools
import math

import jax
import jax.numpy as jnp
import numpy as np
from jax import lax
from jax.experimental import pallas as pl
from jax.experimental.pallas import tpu as pltpu
from jax.sharding import Mesh
from jax.sharding import PartitionSpec as P

HEADS = 8
LANES = 128
NEG = -1e30
NT = (((1,), (1,)), ((), ()))
F32 = jnp.float32
BF16 = jnp.bfloat16


def layer_norm(values, gain):
    center = jnp.mean(values, axis=-1, keepdims=True)
    shifted = values - center
    spread = jnp.mean(shifted * shifted, axis=-1, keepdims=True)
    return shifted * lax.rsqrt(spread + 1e-05) * gain


def pack_stats(peak, total):
    hi = peak.astype(BF16).astype(F32)
    rest = peak - hi
    mid = rest.astype(BF16).astype(F32)
    low = rest - mid
    total_hi = total.astype(BF16).astype(F32)
    total_low = total - total_hi
    group = lax.broadcasted_iota(jnp.int32, peak.shape, 1) // HEADS
    packed = jnp.where(
        group == 0,
        hi,
        jnp.where(
            group == 1,
            mid,
            jnp.where(group == 2, low, jnp.where(group == 3, total_hi, total_low)),
        ),
    )
    return jnp.where(group < 5, packed, 0.0).astype(BF16)


def spread_matrices(width):
    lane = np.arange(LANES)
    columns = np.arange(width + LANES)
    head = np.where(columns < width, columns // (width // HEADS), (columns - width) % HEADS)
    same = (lane[:, None] % HEADS) == head[None, :]
    group = lane[:, None] // HEADS
    peak = same & (group < 3)
    total = same & (group >= 3) & (group < 5)
    return jnp.asarray(peak, BF16), jnp.asarray(total, BF16)


def cross_kernel(
    core_ref,
    queries_ref,
    pos_ref,
    sheets_ref,
    own_ref,
    other_ref,
    own_id_ref,
    other_id_ref,
    level_ref,
    proj_ref,
    out_ref,
    keys,
    values,
    bias,
):
    width = own_ref.shape[1]
    head_size = width // HEADS
    half = own_ref.shape[0]
    levels = level_ref.shape[0]
    pairs = width // LANES

    @pl.when(pl.program_id(0) == 0)
    def _():
        bias[...] = jnp.zeros(bias.shape, bias.dtype)
        lane = lax.broadcasted_iota(jnp.int32, (half, LANES), 1)
        for part, (patch, ids) in enumerate(((own_ref, own_id_ref), (other_ref, other_id_ref))):
            rows = pl.ds(part * half, half)
            columns = ids[...].astype(F32)
            level = jnp.transpose(jnp.broadcast_to(columns[0:1], (LANES, half)))
            sheet = jnp.transpose(jnp.broadcast_to(columns[1:2], (LANES, half)))
            patches = patch[...]
            level = jnp.concatenate([level] * pairs, axis=1)
            added = jnp.zeros((half, width), F32)
            for index in range(levels):
                row = level_ref[index : index + 1].astype(F32)
                added = jnp.where(level == float(index), row, added)
            key_input = (patches.astype(F32) + added).astype(BF16)
            k_all = jnp.dot(key_input, proj_ref[1], preferred_element_type=F32).astype(BF16)
            v_all = jnp.dot(patches, proj_ref[2], preferred_element_type=F32).astype(BF16)
            on_sheet = (sheet == lane.astype(F32)).astype(BF16)
            for head in range(HEADS):
                cut = slice(head // 2 * LANES, head // 2 * LANES + LANES)
                inside = (lane // head_size) == (head % 2)
                keys[head, rows, :LANES] = jnp.where(inside, k_all[:, cut], 0)
                keys[head, rows, LANES:] = on_sheet
                values[head, rows, :LANES] = jnp.where(inside, v_all[:, cut], 0)
                values[head, rows, LANES:] = (lane % HEADS == head).astype(BF16)

    block = queries_ref.shape[0] * queries_ref.shape[1]
    mixed = queries_ref[...].reshape(block, width) + pos_ref[...].reshape(block, width)
    scale = math.log2(math.e) / math.sqrt(head_size)
    q_all = (jnp.dot(mixed, proj_ref[0], preferred_element_type=F32) * scale).astype(BF16)
    sheets = sheets_ref[...].reshape(block, sheets_ref.shape[2])
    bias[:, : sheets_ref.shape[2]] = jnp.where(sheets == 1, 0.0, NEG).astype(BF16)
    barred = bias[...]
    lane = lax.broadcasted_iota(jnp.int32, (block, LANES), 1)
    peaks = jnp.zeros((block, LANES), F32)
    totals = jnp.zeros((block, LANES), F32)
    shape = (out_ref.shape[0], out_ref.shape[1], LANES)
    for pair in range(pairs):
        cut = slice(pair * LANES, pair * LANES + LANES)
        left = jnp.concatenate([q_all[:, cut], barred], axis=1)
        sums = jnp.zeros((block, 2 * LANES), F32)
        for head in (2 * pair, 2 * pair + 1):
            scores = lax.dot_general(left, keys[head], NT, preferred_element_type=F32)
            peak = jnp.max(scores, axis=1, keepdims=True)
            weights = jnp.exp2(scores - peak).astype(BF16)
            sums += jnp.dot(weights, values[head], preferred_element_type=F32)
            peaks = jnp.where(lane % HEADS == head, peak, peaks)
        out_ref[:, :, cut] = sums[:, :LANES].astype(BF16).reshape(shape)
        totals += sums[:, LANES:]
    out_ref[:, :, width:] = pack_stats(peaks, totals).reshape(shape)


def cross_partial(core, queries, query_pos, query_sheets, own, other, own_ids, other_ids, level, proj):
    total, width = queries.shape
    rows = 64
    groups = total // (2 * rows)
    step = 4
    half = own.shape[0]
    sheets = query_sheets.shape[1]
    view = lambda array: array.reshape(groups, 2, rows, array.shape[1])
    by_core = lambda last: pl.BlockSpec(
        (step, None, rows, last), lambda i, core_ref: (i, core_ref[0], 0, 0)
    )
    whole = lambda shape: pl.BlockSpec(shape, lambda i, core_ref: (0,) * len(shape))
    return pl.pallas_call(
        cross_kernel,
        grid_spec=pltpu.PrefetchScalarGridSpec(
            num_scalar_prefetch=1,
            grid=(groups // step,),
            in_specs=[
                by_core(width),
                by_core(width),
                by_core(sheets),
                whole((half, width)),
                whole((half, width)),
                whole((2, half)),
                whole((2, half)),
                whole(level.shape),
                whole((3, width, width)),
            ],
            out_specs=pl.BlockSpec((step, rows, width + LANES), lambda i, core_ref: (i, 0, 0)),
            scratch_shapes=[
                pltpu.VMEM((HEADS, 2 * half, 2 * LANES), BF16),
                pltpu.VMEM((HEADS, 2 * half, 2 * LANES), BF16),
                pltpu.VMEM((step * rows, LANES), BF16),
            ],
        ),
        out_shape=jax.ShapeDtypeStruct((groups, rows, width + LANES), BF16),
        compiler_params=pltpu.CompilerParams(vmem_limit_bytes=48 * 2**20),
        name="cross_partial",
    )(core, view(queries), view(query_pos), view(query_sheets), own, other, own_ids, other_ids, level, proj)


def combine(parts_ref, peak_matrix, total_matrix):
    count, rows, full = parts_ref.shape
    width = full - LANES
    stats = [parts_ref[i, :, width:] for i in range(count)]
    peaks = [jnp.dot(s, peak_matrix, preferred_element_type=F32) for s in stats]
    top = functools.reduce(jnp.maximum, peaks)
    sums = jnp.zeros((rows, width), F32)
    total = jnp.zeros((rows, full), F32)
    for i in range(count):
        factor = jnp.exp2(peaks[i] - top)
        sums += factor[:, :width] * parts_ref[i, :, :width].astype(F32)
        total += factor * jnp.dot(stats[i], total_matrix, preferred_element_type=F32)
    return sums, top, total


def merge_kernel(parts_ref, peak_ref, total_ref, out_ref):
    sums, top, total = combine(parts_ref, peak_ref[...], total_ref[...])
    width = sums.shape[1]
    sums = sums.astype(BF16)
    stats = pack_stats(top[:, width:], total[:, width:])
    for i in range(out_ref.shape[0]):
        out_ref[i, :, :width] = sums
        out_ref[i, :, width:] = stats


def merge(parts, peak_matrix, total_matrix, copies):
    return pl.pallas_call(
        merge_kernel,
        out_shape=jax.ShapeDtypeStruct((copies,) + parts.shape[1:], BF16),
        compiler_params=pltpu.CompilerParams(vmem_limit_bytes=32 * 2**20),
        name="merge",
    )(parts, peak_matrix, total_matrix)


def first_kernel(tile_ref, parts_ref, peak_ref, total_ref, queries_ref, proj_ref, gain_ref, out_ref):
    sums, _, total = combine(parts_ref, peak_ref[...], total_ref[...])
    attended = (sums / total[:, : sums.shape[1]]).astype(BF16)
    crossed = jnp.dot(attended, proj_ref[...], preferred_element_type=F32)
    first = layer_norm(queries_ref[...].astype(F32) + crossed, gain_ref[0:1]).astype(BF16)
    for i in range(out_ref.shape[0]):
        out_ref[i] = first


def first_state_of(tile, parts, peak_matrix, total_matrix, queries, proj, gain, copies):
    _, rows, full = parts.shape
    width = full - LANES
    whole = lambda shape: pl.BlockSpec(shape, lambda i, tile_ref: (0,) * len(shape))
    return pl.pallas_call(
        first_kernel,
        grid_spec=pltpu.PrefetchScalarGridSpec(
            num_scalar_prefetch=1,
            grid=(1,),
            in_specs=[
                whole(parts.shape),
                whole(peak_matrix.shape),
                whole(total_matrix.shape),
                pl.BlockSpec((rows, width), lambda i, tile_ref: (tile_ref[0], 0)),
                pl.BlockSpec((None, width, width), lambda i, tile_ref: (3, 0, 0)),
                whole(gain.shape),
            ],
            out_specs=pl.BlockSpec((copies, rows, width), lambda i, tile_ref: (0, 0, 0)),
        ),
        out_shape=jax.ShapeDtypeStruct((copies, rows, width), BF16),
        compiler_params=pltpu.CompilerParams(vmem_limit_bytes=32 * 2**20),
        name="first_state",
    )(tile, parts, peak_matrix, total_matrix, queries, proj, gain)


def tail_kernel(
    place_ref,
    first_ref,
    own_pos_ref,
    own_ref,
    other_ref,
    pos_a_ref,
    pos_b_ref,
    proj_ref,
    mlp_in_ref,
    mlp_out_ref,
    gain_ref,
    out_ref,
):
    rows, width = first_ref.shape
    head_size = width // HEADS
    keys = own_ref.shape[0] * own_ref.shape[1]
    first = first_ref[...]
    scale = math.log2(math.e) / math.sqrt(head_size)
    q_self = jnp.dot(first + own_pos_ref[...], proj_ref[0], preferred_element_type=F32) * scale
    q_self = q_self.astype(BF16)
    stacked = jnp.concatenate([q_self] * HEADS, axis=0)
    row_head = lax.broadcasted_iota(jnp.int32, stacked.shape, 0) // rows
    col_head = lax.broadcasted_iota(jnp.int32, stacked.shape, 1) // head_size
    mine = row_head == col_head
    stacked = jnp.where(mine, stacked, 0)
    absorbed = lax.dot_general(stacked, proj_ref[1], NT, preferred_element_type=F32).astype(BF16)
    states = [ref[...].reshape(keys, width) for ref in (own_ref, other_ref)]
    inputs = [
        state + ref[...].reshape(keys, width) for state, ref in zip(states, (pos_a_ref, pos_b_ref))
    ]
    scores = [lax.dot_general(absorbed, x, NT, preferred_element_type=F32) for x in inputs]
    peak = functools.reduce(jnp.maximum, [jnp.max(s, axis=1, keepdims=True) for s in scores])
    weights = [jnp.exp2(s - peak) for s in scores]
    total = sum(jnp.sum(w, axis=1, keepdims=True) for w in weights)
    mixed = sum(
        jnp.dot(w.astype(BF16), state, preferred_element_type=F32)
        for w, state in zip(weights, states)
    )
    mixed = (mixed / total).astype(BF16)
    blended = jnp.dot(mixed, proj_ref[2], preferred_element_type=F32)
    blended = jnp.where(mine, blended, 0.0)
    self_out = sum(blended[h * rows : (h + 1) * rows] for h in range(HEADS)).astype(BF16)
    second = first.astype(F32) + jnp.dot(self_out, proj_ref[3], preferred_element_type=F32)
    second = layer_norm(second, gain_ref[1:2]).astype(BF16)
    hidden = jnp.dot(second, mlp_in_ref[...], preferred_element_type=F32)
    hidden = jnp.maximum(hidden, 0.0).astype(BF16)
    decoded = second.astype(F32) + jnp.dot(hidden, mlp_out_ref[...], preferred_element_type=F32)
    out_ref[...] = layer_norm(decoded, gain_ref[2:3]).astype(BF16)


def tail(place, first, own, other, query_pos, proj, mlp_in, mlp_out, gain):
    groups, rows, width = own.shape
    pos = query_pos.reshape(groups, 2, rows, width)
    whole = lambda shape: pl.BlockSpec(shape, lambda i, place_ref: (0,) * len(shape))
    return pl.pallas_call(
        tail_kernel,
        grid_spec=pltpu.PrefetchScalarGridSpec(
            num_scalar_prefetch=1,
            grid=(1,),
            in_specs=[
                pl.BlockSpec((None, rows, width), lambda i, place_ref: (0, 0, 0)),
                pl.BlockSpec((rows, width), lambda i, place_ref: (place_ref[1], 0)),
                whole(own.shape),
                whole(other.shape),
                pl.BlockSpec((groups, None, rows, width), lambda i, place_ref: (0, place_ref[0], 0, 0)),
                pl.BlockSpec(
                    (groups, None, rows, width), lambda i, place_ref: (0, 1 - place_ref[0], 0, 0)
                ),
                whole(proj.shape),
                whole(mlp_in.shape),
                whole(mlp_out.shape),
                whole(gain.shape),
            ],
            out_specs=pl.BlockSpec((rows, width), lambda i, place_ref: (0, 0)),
        ),
        out_shape=jax.ShapeDtypeStruct((rows, width), BF16),
        compiler_params=pltpu.CompilerParams(vmem_limit_bytes=56 * 2**20),
        name="tail",
    )(place, first, query_pos, own, other, pos, pos, proj, mlp_in, mlp_out, gain)


def body(
    queries,
    query_pos,
    patches,
    patch_level,
    patch_sheet,
    query_sheets,
    level_embed,
    cross_proj,
    self_proj,
    mlp_in,
    mlp_out,
    norm_gain,
):
    core = lax.axis_index("c").astype(jnp.int32)
    square = lax.axis_size("x") * lax.axis_size("y")
    bands = lax.axis_size("z")
    tile = (lax.axis_index("x") * lax.axis_size("y") + lax.axis_index("y")) * 2 + core
    place = jnp.stack([core, tile.astype(jnp.int32)])
    swap = [(0, 1), (1, 0)]
    ids = jnp.stack([patch_level, patch_sheet])
    other_patches = lax.ppermute(patches, "c", swap)
    other_ids = lax.ppermute(ids, "c", swap)
    peak_matrix, total_matrix = spread_matrices(queries.shape[1])
    parts = cross_partial(
        place,
        queries,
        query_pos,
        query_sheets,
        patches,
        other_patches,
        ids,
        other_ids,
        level_embed,
        cross_proj[:3],
    )
    parts = lax.all_to_all(parts, ("x", "y"), 0, 0, tiled=True)
    parts = merge(parts, peak_matrix, total_matrix, bands)
    parts = lax.all_to_all(parts, "z", 0, 0, tiled=True)
    first = first_state_of(
        place[1:], parts, peak_matrix, total_matrix, queries, cross_proj, norm_gain, square
    )
    own = lax.all_to_all(first, ("x", "y"), 0, 0, tiled=True)
    other = lax.ppermute(own, "c", swap)
    return tail(place, first, own, other, query_pos, self_proj, mlp_in, mlp_out, norm_gain)


def solution(mesh):
    devices = mesh.devices
    grid = Mesh(devices.reshape(devices.shape[0], 4, 4, 2), ("z", "x", "y", "c"))
    every = ("z", "x", "y", "c")
    return jax.shard_map(
        body,
        mesh=grid,
        in_specs=(
            P(),
            P(),
            P(every, None),
            P(every),
            P(every),
            P(),
            P(),
            P(),
            P(),
            P(),
            P(),
            P(),
        ),
        out_specs=P(("x", "y", "c"), None),
        check_vma=False,
    )
```

```python
import functools
import math

import jax
import jax.numpy as jnp
import numpy as np
from jax import lax
from jax.experimental import pallas as pl
from jax.experimental.pallas import tpu as pltpu
from jax.sharding import Mesh
from jax.sharding import PartitionSpec as P

HEADS = 8
LANES = 128
NEG = -1e30
SMALL = 32 * 2**20
LARGE = 60 * 2**20
NT = (((1,), (1,)), ((), ()))
F32 = jnp.float32
BF16 = jnp.bfloat16


def layer_norm(values, gain):
    center = jnp.mean(values, axis=-1, keepdims=True)
    shifted = values - center
    spread = jnp.mean(shifted * shifted, axis=-1, keepdims=True)
    return shifted * lax.rsqrt(spread + 1e-05) * gain


def pack_stats(peak, total):
    hi = peak.astype(BF16).astype(F32)
    rest = peak - hi
    mid = rest.astype(BF16).astype(F32)
    low = rest - mid
    total_hi = total.astype(BF16).astype(F32)
    total_low = total - total_hi
    group = lax.broadcasted_iota(jnp.int32, peak.shape, 1) // HEADS
    packed = jnp.where(
        group == 0,
        hi,
        jnp.where(
            group == 1,
            mid,
            jnp.where(group == 2, low, jnp.where(group == 3, total_hi, total_low)),
        ),
    )
    return jnp.where(group < 5, packed, 0.0).astype(BF16)


def spread_matrices(width):
    lane = np.arange(LANES)
    columns = np.arange(width + LANES)
    head = np.where(columns < width, columns // (width // HEADS), (columns - width) % HEADS)
    same = (lane[:, None] % HEADS) == head[None, :]
    group = lane[:, None] // HEADS
    peak = same & (group < 3)
    total = same & (group >= 3) & (group < 5)
    return jnp.asarray(peak, BF16), jnp.asarray(total, BF16)


def project_patches(patches, level_ids, sheet_ids, level_ref, w_key, w_value):
    rows, width = patches.shape
    spread = lambda ids: jnp.transpose(
        jnp.broadcast_to(ids.reshape(1, rows).astype(F32), (LANES, rows))
    )
    level = jnp.concatenate([spread(level_ids)] * (width // LANES), axis=1)
    added = jnp.zeros((rows, width), F32)
    for index in range(level_ref.shape[0]):
        added = jnp.where(level == float(index), level_ref[index : index + 1].astype(F32), added)
    key_input = (patches.astype(F32) + added).astype(BF16)
    keys = jnp.dot(key_input, w_key, preferred_element_type=F32).astype(BF16)
    values = jnp.dot(patches, w_value, preferred_element_type=F32).astype(BF16)
    lane = lax.broadcasted_iota(jnp.int32, (rows, LANES), 1)
    return keys, values, (spread(sheet_ids) == lane.astype(F32)).astype(BF16)


def start_all(pairs, sems):
    loads = [
        pltpu.make_async_copy(source, target, sems.at[i]) for i, (source, target) in enumerate(pairs)
    ]
    for load in loads:
        load.start()
    return loads


def cross_kernel(
    level_a_hbm,
    sheet_a_hbm,
    level_b_hbm,
    sheet_b_hbm,
    level_hbm,
    sheets_hbm,
    patch_a_hbm,
    patch_b_hbm,
    queries_hbm,
    pos_hbm,
    proj_hbm,
    out_hbm,
    ids,
    level_ref,
    sheets_ref,
    out_ref,
    patches,
    queries,
    pos,
    proj,
    key_ref,
    value_ref,
    on_ref,
    sems,
    out_sems,
):
    core = lax.axis_index("c")
    groups, rows, width = queries.shape
    half = patch_a_hbm.shape[0]
    block = groups * rows
    head_size = width // HEADS
    loads = start_all(
        (
            (sheets_hbm, sheets_ref),
            (level_hbm, level_ref),
            (level_a_hbm, ids.at[0]),
            (sheet_a_hbm, ids.at[1]),
            (level_b_hbm, ids.at[2]),
            (sheet_b_hbm, ids.at[3]),
            (proj_hbm.at[pl.ds(1, 2)], proj.at[pl.ds(1, 2)]),
            (patch_a_hbm, patches.at[0]),
            (patch_b_hbm, patches.at[1]),
            (proj_hbm.at[0], proj.at[0]),
            (queries_hbm.at[:, core], queries),
            (pos_hbm.at[:, core], pos),
        ),
        sems,
    )
    loads[0].wait()
    sheets = sheets_ref.shape[0]
    barred = jnp.where(sheets_ref[...] == 1, 0.0, NEG)
    barred = jnp.concatenate([barred, jnp.zeros((LANES - sheets, 2 * block), F32)], axis=0)
    barred = jnp.transpose(barred).reshape(groups, 2, rows, LANES)
    barred = jnp.where(core == 0, barred[:, 0], barred[:, 1])
    barred = barred.reshape(block, LANES).astype(BF16)
    for load in loads[1:7]:
        load.wait()
    for i in range(2):
        loads[7 + i].wait()
        cut = pl.ds(i * half, half)
        key_ref[cut], value_ref[cut], on_ref[cut] = project_patches(
            patches[i], ids[2 * i], ids[2 * i + 1], level_ref, proj[1], proj[2]
        )
    for load in loads[9:]:
        load.wait()
    mixed = queries[...].reshape(block, width) + pos[...].reshape(block, width)
    scale = math.log2(math.e) / math.sqrt(head_size)
    q_all = (jnp.dot(mixed, proj[0], preferred_element_type=F32) * scale).astype(BF16)
    lane = lax.broadcasted_iota(jnp.int32, (block, LANES), 1)
    ones = jnp.ones((2 * half, LANES), BF16)
    peaks = jnp.zeros((block, LANES), F32)
    totals = jnp.zeros((block, LANES), F32)
    shape = (groups, rows, LANES)

    def score(head):
        cut = slice(head // 2 * LANES, head // 2 * LANES + LANES)
        inside = lane // head_size == head % 2
        left = jnp.concatenate([jnp.where(inside, q_all[:, cut], 0), barred], axis=1)
        right = jnp.concatenate([key_ref[:, cut], on_ref[...]], axis=1)
        return lax.dot_general(left, right, NT, preferred_element_type=F32)

    def store(cut):
        copy = pltpu.make_async_copy(
            out_ref.at[:, :, cut], out_hbm.at[:, :, cut], out_sems.at[cut.start // LANES]
        )
        copy.start()
        return copy

    scores = score(0)
    stores = []
    sums = None
    for head in range(HEADS):
        now, scores = scores, score(head + 1) if head + 1 < HEADS else None
        cut = slice(head // 2 * LANES, head // 2 * LANES + LANES)
        peak = jnp.max(now, axis=1, keepdims=True)
        weights = jnp.exp2(now - peak).astype(BF16)
        values = jnp.concatenate([value_ref[:, cut], ones], axis=1)
        part = jnp.dot(weights, values, preferred_element_type=F32)
        here = lane % HEADS == head
        peaks = jnp.where(here, peak, peaks)
        totals = jnp.where(here, part[:, LANES:], totals)
        if head % 2 == 0:
            sums = part[:, :LANES]
        else:
            sums = jnp.where(lane // head_size == 0, sums, part[:, :LANES])
            out_ref[:, :, cut] = sums.astype(BF16).reshape(shape)
            stores.append(store(cut))
    out_ref[:, :, width:] = pack_stats(peaks, totals).reshape(shape)
    stores.append(store(slice(width, width + LANES)))
    for copy in stores:
        copy.wait()


def cross_partial(queries, query_pos, query_sheets, own, other, level, proj):
    total, width = queries.shape
    rows = 64
    groups = total // (2 * rows)
    half = own[0].shape[0]
    view = lambda array: array.reshape(groups, 2, rows, array.shape[1])
    hbm = pl.BlockSpec(memory_space=pltpu.HBM)
    return pl.pallas_call(
        cross_kernel,
        in_specs=[hbm] * 11,
        out_specs=hbm,
        scratch_shapes=[
            pltpu.VMEM((4, half), jnp.int32),
            pltpu.VMEM(level.shape, BF16),
            pltpu.VMEM(query_sheets.shape[::-1], jnp.int32),
            pltpu.VMEM((groups, rows, width + LANES), BF16),
            pltpu.VMEM((2, half, width), BF16),
            pltpu.VMEM((groups, rows, width), BF16),
            pltpu.VMEM((groups, rows, width), BF16),
            pltpu.VMEM((3, width, width), BF16),
            pltpu.VMEM((2 * half, width), BF16),
            pltpu.VMEM((2 * half, width), BF16),
            pltpu.VMEM((2 * half, LANES), BF16),
            pltpu.SemaphoreType.DMA((12,)),
            pltpu.SemaphoreType.DMA((width // LANES + 1,)),
        ],
        out_shape=jax.ShapeDtypeStruct((groups, rows, width + LANES), BF16),
        compiler_params=pltpu.CompilerParams(vmem_limit_bytes=LARGE),
        name="cross_partial",
    )(
        *own[1:],
        *other[1:],
        level,
        query_sheets.T,
        own[0],
        other[0],
        view(queries),
        view(query_pos),
        proj,
    )


def combine(parts, peak_matrix, total_matrix):
    width = parts[0].shape[1] - LANES
    stats = [part[:, width:] for part in parts]
    peaks = [jnp.dot(s, peak_matrix, preferred_element_type=F32) for s in stats]
    top = functools.reduce(jnp.maximum, peaks)
    factors = [jnp.exp2(peak - top) for peak in peaks]
    sums = [f[:, :width] * part[:, :width].astype(F32) for f, part in zip(factors, parts)]
    totals = [
        f * jnp.dot(s, total_matrix, preferred_element_type=F32) for f, s in zip(factors, stats)
    ]

    def tree(terms):
        while len(terms) > 1:
            terms = [sum(terms[i : i + 2]) for i in range(0, len(terms), 2)]
        return terms[0]

    return tree(sums), top, tree(totals)


def packed(sums, top, total):
    width = sums.shape[1]
    return jnp.concatenate(
        [sums.astype(BF16), pack_stats(top[:, width:], total[:, width:])], axis=1
    )


def merge_kernel(parts_ref, peak_ref, total_ref, out_ref):
    parts = [parts_ref[i] for i in range(parts_ref.shape[0])]
    out_ref[...] = packed(*combine(parts, peak_ref[...], total_ref[...]))


def merge_two_kernel(a_ref, b_ref, peak_ref, total_ref, out_ref):
    out_ref[...] = packed(*combine([a_ref[...], b_ref[...]], peak_ref[...], total_ref[...]))


def merge(kernel, shape, *operands):
    return pl.pallas_call(
        kernel,
        out_shape=jax.ShapeDtypeStruct(shape, BF16),
        compiler_params=pltpu.CompilerParams(vmem_limit_bytes=SMALL),
        name="merge",
    )(*operands)


def column():
    return lax.axis_index("x") * lax.axis_size("y") + lax.axis_index("y")


def first_kernel(
    a_ref,
    b_ref,
    c_ref,
    d_ref,
    peak_ref,
    total_ref,
    queries_hbm,
    proj_hbm,
    gain_ref,
    out_ref,
    queries,
    weights,
    sems,
):
    loads = start_all(
        ((proj_hbm.at[3], weights), (queries_hbm.at[column(), lax.axis_index("c")], queries)), sems
    )
    parts = [ref[...] for ref in (a_ref, b_ref, c_ref, d_ref)]
    sums, _, total = combine(parts, peak_ref[...], total_ref[...])
    attended = (sums / total[:, : sums.shape[1]]).astype(BF16)
    for load in loads:
        load.wait()
    crossed = jnp.dot(attended, weights[...], preferred_element_type=F32)
    first = layer_norm(queries[...].astype(F32) + crossed, gain_ref[0:1]).astype(BF16)
    for i in range(out_ref.shape[0]):
        out_ref[i] = first


def first_state_of(parts, peak_matrix, total_matrix, queries, proj, gain, copies):
    rows, full = parts[0].shape
    width = full - LANES
    local = pl.BlockSpec(memory_space=pltpu.VMEM)
    hbm = pl.BlockSpec(memory_space=pltpu.HBM)
    return pl.pallas_call(
        first_kernel,
        in_specs=[local] * 6 + [hbm, hbm, local],
        out_specs=local,
        scratch_shapes=[
            pltpu.VMEM((rows, width), BF16),
            pltpu.VMEM((width, width), BF16),
            pltpu.SemaphoreType.DMA((2,)),
        ],
        out_shape=jax.ShapeDtypeStruct((copies, rows, width), BF16),
        compiler_params=pltpu.CompilerParams(vmem_limit_bytes=SMALL),
        name="first_state",
    )(
        *parts,
        peak_matrix,
        total_matrix,
        queries.reshape(copies, 2, rows, width),
        proj,
        gain,
    )


def stack_heads(array, rows):
    stacked = jnp.concatenate([array] * HEADS, axis=0)
    row_head = lax.broadcasted_iota(jnp.int32, stacked.shape, 0) // rows
    col_head = lax.broadcasted_iota(jnp.int32, stacked.shape, 1) // (stacked.shape[1] // HEADS)
    mine = row_head == col_head
    return jnp.where(mine, stacked, 0), mine


def near_kernel(
    first_ref,
    state_ref,
    pos_hbm,
    proj_hbm,
    absorbed_ref,
    mixed_ref,
    stat_ref,
    own_pos,
    pos,
    weights,
    sems,
):
    groups, rows, width = state_ref.shape
    core = lax.axis_index("c")
    loads = start_all(
        (
            (proj_hbm.at[pl.ds(0, 2)], weights),
            (pos_hbm.at[column(), core], own_pos),
            (pos_hbm.at[:, core], pos),
        ),
        sems,
    )
    for load in loads[:2]:
        load.wait()
    scale = math.log2(math.e) / math.sqrt(width // HEADS)
    self_in = first_ref[0] + own_pos[...]
    q_self = jnp.dot(self_in, weights[0], preferred_element_type=F32) * scale
    stacked, _ = stack_heads(q_self.astype(BF16), rows)
    absorbed = lax.dot_general(stacked, weights[1], NT, preferred_element_type=F32).astype(BF16)
    absorbed_ref[...] = absorbed
    state = state_ref[...].reshape(groups * rows, width)
    loads[2].wait()
    inputs = state + pos[...].reshape(groups * rows, width)
    scores = lax.dot_general(absorbed, inputs, NT, preferred_element_type=F32)
    peak = jnp.max(scores, axis=1, keepdims=True)
    weights_here = jnp.exp2(scores - peak)
    total = jnp.sum(weights_here, axis=1, keepdims=True)
    mixed_ref[...] = jnp.dot(weights_here.astype(BF16), state, preferred_element_type=F32)
    lane = lax.broadcasted_iota(jnp.int32, stat_ref.shape, 1)
    stat_ref[...] = jnp.where(lane == 0, peak, total)


def near_half(first, own, query_pos, proj):
    groups, rows, width = own.shape
    local = pl.BlockSpec(memory_space=pltpu.VMEM)
    hbm = pl.BlockSpec(memory_space=pltpu.HBM)
    shapes = [(HEADS * rows, width), (HEADS * rows, width), (HEADS * rows, LANES)]
    return pl.pallas_call(
        near_kernel,
        in_specs=[local, local, hbm, hbm],
        out_specs=[local] * 3,
        scratch_shapes=[
            pltpu.VMEM((rows, width), BF16),
            pltpu.VMEM(own.shape, BF16),
            pltpu.VMEM((2, width, width), BF16),
            pltpu.SemaphoreType.DMA((3,)),
        ],
        out_shape=[
            jax.ShapeDtypeStruct(shape, kind) for shape, kind in zip(shapes, (BF16, F32, F32))
        ],
        compiler_params=pltpu.CompilerParams(vmem_limit_bytes=SMALL),
        cost_estimate=pl.CostEstimate(
            flops=2**33, bytes_accessed=2**22, transcendentals=2**20
        ),
        name="near_half",
    )(first, own, query_pos.reshape(groups, 2, rows, width), proj)


def tail_kernel(
    first_ref,
    absorbed_ref,
    mixed_ref,
    stat_ref,
    state_ref,
    pos_hbm,
    proj_hbm,
    mlp_in_hbm,
    mlp_out_hbm,
    gain_ref,
    out_ref,
    pos,
    proj_ref,
    mlp_in_ref,
    mlp_out_ref,
    sems,
):
    loads = start_all(
        (
            (pos_hbm.at[:, 1 - lax.axis_index("c")], pos),
            (proj_hbm.at[pl.ds(2, 2)], proj_ref),
            (mlp_in_hbm, mlp_in_ref),
            (mlp_out_hbm, mlp_out_ref),
        ),
        sems,
    )
    _, rows, width = first_ref.shape
    keys = state_ref.shape[0] * state_ref.shape[1]
    state = state_ref[...].reshape(keys, width)
    loads[0].wait()
    inputs = state + pos[...].reshape(keys, width)
    scores = lax.dot_general(absorbed_ref[...], inputs, NT, preferred_element_type=F32)
    peak_a, total_a = stat_ref[:, 0:1], stat_ref[:, 1:2]
    peak_b = jnp.max(scores, axis=1, keepdims=True)
    peak = jnp.maximum(peak_a, peak_b)
    weights = jnp.exp2(scores - peak)
    factor = jnp.exp2(peak_a - peak)
    total = factor * total_a + jnp.sum(weights, axis=1, keepdims=True)
    mixed = factor * mixed_ref[...]
    mixed += jnp.dot(weights.astype(BF16), state, preferred_element_type=F32)
    mixed = (mixed / total).astype(BF16)
    loads[1].wait()
    blended = jnp.dot(mixed, proj_ref[0], preferred_element_type=F32)
    head_size = width // HEADS
    column = lax.broadcasted_iota(jnp.int32, (rows, width), 1) // head_size
    self_out = jnp.zeros((rows, width), F32)
    for head in range(HEADS):
        self_out = jnp.where(column == head, blended[head * rows : (head + 1) * rows], self_out)
    second = first_ref[0].astype(F32) + jnp.dot(
        self_out.astype(BF16), proj_ref[1], preferred_element_type=F32
    )
    second = layer_norm(second, gain_ref[1:2]).astype(BF16)
    loads[2].wait()
    hidden = jnp.dot(second, mlp_in_ref[...], preferred_element_type=F32)
    hidden = jnp.maximum(hidden, 0.0).astype(BF16)
    loads[3].wait()
    decoded = second.astype(F32) + jnp.dot(hidden, mlp_out_ref[...], preferred_element_type=F32)
    out_ref[...] = layer_norm(decoded, gain_ref[2:3]).astype(BF16)


def tail(first, partial, other, query_pos, proj, mlp_in, mlp_out, gain):
    groups, rows, width = other.shape
    local = pl.BlockSpec(memory_space=pltpu.VMEM)
    hbm = pl.BlockSpec(memory_space=pltpu.HBM)
    return pl.pallas_call(
        tail_kernel,
        in_specs=[local] * 5 + [hbm] * 4 + [local],
        out_specs=local,
        scratch_shapes=[
            pltpu.VMEM(other.shape, BF16),
            pltpu.VMEM((2, width, width), BF16),
            pltpu.VMEM(mlp_in.shape, BF16),
            pltpu.VMEM(mlp_out.shape, BF16),
            pltpu.SemaphoreType.DMA((4,)),
        ],
        out_shape=jax.ShapeDtypeStruct((rows, width), BF16),
        compiler_params=pltpu.CompilerParams(vmem_limit_bytes=SMALL),
        name="tail",
    )(
        first,
        *partial,
        other,
        query_pos.reshape(groups, 2, rows, width),
        proj,
        mlp_in,
        mlp_out,
        gain,
    )


def body(
    queries,
    query_pos,
    patches,
    patch_level,
    patch_sheet,
    query_sheets,
    level_embed,
    cross_proj,
    self_proj,
    mlp_in,
    mlp_out,
    norm_gain,
):
    square = lax.axis_size("x") * lax.axis_size("y")
    bands = lax.axis_size("z")
    swap = [(0, 1), (1, 0)]
    own = (patches, patch_level, patch_sheet)
    other = [lax.ppermute(array, "c", swap) for array in own]
    spread = spread_matrices(queries.shape[1])
    parts = cross_partial(queries, query_pos, query_sheets, own, other, level_embed, cross_proj)
    parts = lax.all_to_all(parts, ("x", "y"), 0, 0, tiled=True)
    part = merge(merge_kernel, parts.shape[1:], parts, *spread)
    part = merge(
        merge_two_kernel,
        part.shape,
        part,
        lax.ppermute(part, "z", [(i, i ^ 1) for i in range(bands)]),
        *spread,
    )
    sign = lambda i: 1 - 2 * (i % 2)
    shift = lambda hop: lax.ppermute(
        part, "z", [(i, (i + hop * sign(i)) % bands) for i in range(bands)]
    )
    near, middle, far = shift(-1), shift(-2), shift(-3)
    first = first_state_of(
        (part, far, near, middle),
        *spread,
        queries,
        cross_proj,
        norm_gain,
        square,
    )
    own = lax.all_to_all(first, ("x", "y"), 0, 0, tiled=True)
    other = lax.ppermute(own, "c", swap)
    partial = near_half(first, own, query_pos, self_proj)
    return tail(first, partial, other, query_pos, self_proj, mlp_in, mlp_out, norm_gain)


def solution(mesh):
    devices = mesh.devices
    names = ("z", "x", "y", "c")
    grid = Mesh(devices.reshape(devices.shape[0], 4, 4, 2), names)
    return jax.shard_map(
        body,
        mesh=grid,
        in_specs=(P(), P(), P(names, None), P(names), P(names)) + (P(),) * 7,
        out_specs=P(names[1:], None),
        check_vma=False,
    )
```

```python
import functools
import math

import jax
import jax.numpy as jnp
from jax import lax
from jax.experimental import pallas as pl
from jax.experimental.pallas import tpu as pltpu
from jax.sharding import Mesh
from jax.sharding import PartitionSpec as P

HEADS = 8
LANES = 128
NEG = -1e30
SMALL = 32 * 2**20
LARGE = 63_400_000
NT = (((1,), (1,)), ((), ()))
F32 = jnp.float32
BF16 = jnp.bfloat16


def layer_norm(values, gain):
    center = jnp.mean(values, axis=-1, keepdims=True)
    shifted = values - center
    spread = jnp.mean(shifted * shifted, axis=-1, keepdims=True)
    return shifted * lax.rsqrt(spread + 1e-05) * gain


def pieces(value):
    hi = value.astype(BF16).astype(F32)
    mid = (value - hi).astype(BF16).astype(F32)
    return hi, mid, value - hi - mid


def project_patches(patches, level_ids, sheet_ids, sheets, level_rows, w_key, w_value):
    rows, width = patches.shape
    row = lax.broadcasted_iota(jnp.int32, (LANES, rows), 0)
    held = (row == sheet_ids.reshape(1, rows)) | (row == level_ids.reshape(1, rows) + sheets)
    held = jnp.transpose(jnp.where(held, 1.0, 0.0)).astype(BF16)
    added = jnp.dot(held, level_rows, preferred_element_type=F32)
    key_input = (patches.astype(F32) + added).astype(BF16)
    keys = jnp.dot(key_input, w_key, preferred_element_type=F32).astype(BF16)
    values = jnp.dot(patches, w_value, preferred_element_type=F32).astype(BF16)
    return keys, values, held


def start_all(pairs, sems):
    loads = [
        pltpu.make_async_copy(source, target, sems.at[i]) for i, (source, target) in enumerate(pairs)
    ]
    for load in loads:
        load.start()
    return loads


def cross_kernel(
    level_a_hbm,
    sheet_a_hbm,
    level_b_hbm,
    sheet_b_hbm,
    level_hbm,
    sheets_hbm,
    patch_a_hbm,
    patch_b_hbm,
    queries_hbm,
    pos_hbm,
    proj_hbm,
    out_hbm,
    ids,
    level_ref,
    sheets_ref,
    out_ref,
    patches,
    queries,
    pos,
    proj,
    key_ref,
    value_ref,
    on_ref,
    sems,
    out_sems,
):
    core = lax.axis_index("c")
    groups, rows, width = queries.shape
    half = patch_a_hbm.shape[0]
    block = groups * rows
    head_size = width // HEADS
    loads = start_all(
        (
            (sheets_hbm, sheets_ref),
            (level_hbm, level_ref),
            (level_a_hbm, ids.at[0]),
            (sheet_a_hbm, ids.at[1]),
            (level_b_hbm, ids.at[2]),
            (sheet_b_hbm, ids.at[3]),
            (proj_hbm.at[pl.ds(1, 2)], proj.at[pl.ds(1, 2)]),
            (patch_a_hbm, patches.at[0]),
            (patch_b_hbm, patches.at[1]),
            (proj_hbm.at[0], proj.at[0]),
            (queries_hbm.at[:, core], queries),
            (pos_hbm.at[:, core], pos),
        ),
        sems,
    )
    loads[0].wait()
    sheets = sheets_ref.shape[0]
    cut = lax.broadcasted_iota(jnp.int32, (sheets, LANES), 1) < rows
    picked = []
    for start in range(0, 2 * block, 2 * LANES):
        even = sheets_ref[:, start : start + LANES]
        odd = sheets_ref[:, start + LANES : start + 2 * LANES]
        low = jnp.where(cut, even, pltpu.roll(odd, rows, 1))
        high = jnp.where(cut, pltpu.roll(even, rows, 1), odd)
        picked.append(jnp.where(core == 0, low, high))
    barred = jnp.where(jnp.concatenate(picked, axis=1) == 1, 0.0, NEG)
    barred = jnp.concatenate([barred, jnp.zeros((LANES - sheets, block), F32)], axis=0)
    barred = jnp.transpose(barred).astype(BF16)
    for load in loads[1:7]:
        load.wait()
    row = lax.broadcasted_iota(jnp.int32, (LANES, width), 0)
    level_rows = jnp.zeros((LANES, width), F32)
    for index in range(level_ref.shape[0]):
        added = level_ref[index : index + 1].astype(F32)
        level_rows = jnp.where(row == sheets + index, added, level_rows)
    level_rows = level_rows.astype(BF16)
    for i in range(2):
        loads[7 + i].wait()
        cut = pl.ds(i * half, half)
        key_ref[cut], value_ref[cut], on_ref[cut] = project_patches(
            patches[i], ids[2 * i], ids[2 * i + 1], sheets, level_rows, proj[1], proj[2]
        )
    for load in loads[9:]:
        load.wait()
    mixed = queries[...].reshape(block, width) + pos[...].reshape(block, width)
    scale = math.log2(math.e) / math.sqrt(head_size)
    q_all = (jnp.dot(mixed, proj[0], preferred_element_type=F32) * scale).astype(BF16)
    lane = lax.broadcasted_iota(jnp.int32, (block, LANES), 1)
    ones = jnp.ones((2 * half, LANES), BF16)
    peaks = jnp.zeros((block, LANES), F32)
    totals = jnp.zeros((block, LANES), F32)

    def score(head):
        cut = slice(head // 2 * LANES, head // 2 * LANES + LANES)
        inside = lane // head_size == head % 2
        left = jnp.concatenate([jnp.where(inside, q_all[:, cut], 0), barred], axis=1)
        right = jnp.concatenate([key_ref[:, cut], on_ref[...]], axis=1)
        return lax.dot_general(left, right, NT, preferred_element_type=F32)

    def store(cut):
        copy = pltpu.make_async_copy(
            out_ref.at[:, :, cut], out_hbm.at[:, :, cut], out_sems.at[cut.start // LANES]
        )
        copy.start()
        return copy

    scores = score(0)
    sums = None
    for head in range(HEADS):
        now, scores = scores, score(head + 1) if head + 1 < HEADS else None
        cut = slice(head // 2 * LANES, head // 2 * LANES + LANES)
        peak = jnp.max(now, axis=1, keepdims=True)
        weights = jnp.exp2(now - peak).astype(BF16)
        values = jnp.concatenate([value_ref[:, cut], ones], axis=1)
        part = jnp.dot(weights, values, preferred_element_type=F32)
        here = lane % HEADS == head
        peaks = jnp.where(here, peak, peaks)
        totals = jnp.where(here, part[:, LANES:], totals)
        if head % 2 == 0:
            sums = part[:, :LANES]
        else:
            sums = jnp.where(lane // head_size == 0, sums, part[:, :LANES])
            sums = sums.astype(BF16).reshape(groups, rows, LANES)
            for group in range(groups):
                out_ref[group, :rows, cut] = sums[group]
    kind = lane // HEADS
    hi, mid, low = pieces(peaks)
    stats = jnp.where(kind == 0, hi, jnp.where(kind == 1, mid, jnp.where(kind == 2, low, totals)))
    stats = jnp.transpose(stats)
    for group in range(0, groups, 2):
        cut = slice(group * rows, group * rows + LANES)
        tile = [stats[k * HEADS : k * HEADS + HEADS, cut] for k in range(width // LANES)]
        tile = jnp.concatenate(tile, axis=1).astype(BF16)
        out_ref[group, rows:] = tile
        out_ref[group + 1, rows:] = tile
    stores = [store(slice(i, i + LANES)) for i in range(0, width, LANES)]
    for copy in stores:
        copy.wait()


def cross_partial(queries, query_pos, query_sheets, own, other, level, proj):
    total, width = queries.shape
    rows = 64
    groups = total // (2 * rows)
    half = own[0].shape[0]
    view = lambda array: array.reshape(groups, 2, rows, array.shape[1])
    hbm = pl.BlockSpec(memory_space=pltpu.HBM)
    return pl.pallas_call(
        cross_kernel,
        in_specs=[hbm] * 11,
        out_specs=hbm,
        scratch_shapes=[
            pltpu.VMEM((4, half), jnp.int32),
            pltpu.VMEM(level.shape, BF16),
            pltpu.VMEM(query_sheets.shape[::-1], jnp.int32),
            pltpu.VMEM((groups, rows + HEADS, width), BF16),
            pltpu.VMEM((2, half, width), BF16),
            pltpu.VMEM((groups, rows, width), BF16),
            pltpu.VMEM((groups, rows, width), BF16),
            pltpu.VMEM((3, width, width), BF16),
            pltpu.VMEM((2 * half, width), BF16),
            pltpu.VMEM((2 * half, width), BF16),
            pltpu.VMEM((2 * half, LANES), BF16),
            pltpu.SemaphoreType.DMA((12,)),
            pltpu.SemaphoreType.DMA((width // LANES,)),
        ],
        out_shape=jax.ShapeDtypeStruct((groups, rows + HEADS, width), BF16),
        compiler_params=pltpu.CompilerParams(vmem_limit_bytes=LARGE),
        name="cross_partial",
    )(
        *own[1:],
        *other[1:],
        level,
        query_sheets.T,
        own[0],
        other[0],
        view(queries),
        view(query_pos),
        proj,
    )


def by_row(table, rows):
    if table.shape[0] < LANES:
        rest = jnp.zeros((LANES - table.shape[0], LANES), F32)
        table = jnp.concatenate([table, rest], axis=0)
    table = jnp.transpose(table)
    odd = lax.rem(column(), 2)
    return jnp.where(odd == 0, table[:rows], table[rows : 2 * rows])


def head_columns(width):
    shape = (LANES, width)
    head = lax.broadcasted_iota(jnp.int32, shape, 1) // (width // HEADS)
    same = lax.broadcasted_iota(jnp.int32, shape, 0) == head
    return jnp.where(same, 1.0, 0.0).astype(BF16)


def tree(terms):
    while len(terms) > 1:
        terms = [sum(terms[i : i + 2]) for i in range(0, len(terms), 2)]
    return terms[0]


def combine(refs):
    rows, width = refs[0].shape[0] - HEADS, refs[0].shape[1]
    stats = [ref[rows:].astype(F32) for ref in refs]
    cut = lambda s, k: s[:, k * LANES : k * LANES + LANES]
    peaks = [cut(s, 0) + cut(s, 1) + cut(s, 2) for s in stats]
    top = functools.reduce(jnp.maximum, peaks)
    factors = [jnp.exp2(peak - top).astype(BF16).astype(F32) for peak in peaks]
    total = tree([f * cut(s, 3) for f, s in zip(factors, stats)])
    table = by_row(jnp.concatenate(factors, axis=0), rows)
    spread = head_columns(width)
    sums = []
    for i, ref in enumerate(refs):
        factor = table if i == 0 else pltpu.roll(table, LANES - i * HEADS, 1)
        factor = jnp.dot(factor.astype(BF16), spread, preferred_element_type=F32)
        sums.append(factor * ref[:rows].astype(F32))
    return tree(sums), top, total


def write_merged(out_ref, sums, top, total):
    rows = sums.shape[0]
    out_ref[:rows] = sums.astype(BF16)
    out_ref[rows:] = jnp.concatenate([*pieces(top), total], axis=1).astype(BF16)


def merge_kernel(parts_ref, out_ref):
    write_merged(out_ref, *combine([parts_ref.at[i] for i in range(parts_ref.shape[0])]))


def merge_two_kernel(a_ref, b_ref, out_ref):
    write_merged(out_ref, *combine([a_ref, b_ref]))


def merge(kernel, shape, *operands):
    return pl.pallas_call(
        kernel,
        out_shape=jax.ShapeDtypeStruct(shape, BF16),
        compiler_params=pltpu.CompilerParams(vmem_limit_bytes=SMALL),
        name="merge",
    )(*operands)


def column():
    return lax.axis_index("x") * lax.axis_size("y") + lax.axis_index("y")


def first_kernel(
    a_ref,
    b_ref,
    c_ref,
    d_ref,
    queries_hbm,
    proj_hbm,
    gain_ref,
    out_ref,
    queries,
    weights,
    sems,
):
    loads = start_all(
        ((proj_hbm.at[3], weights), (queries_hbm.at[column(), lax.axis_index("c")], queries)), sems
    )
    sums, _, total = combine([a_ref, b_ref, c_ref, d_ref])
    rows, width = sums.shape
    spread = head_columns(width)
    total = tree(
        [
            jnp.dot(by_row(piece, rows).astype(BF16), spread, preferred_element_type=F32)
            for piece in pieces(total)
        ]
    )
    attended = (sums / total).astype(BF16)
    for load in loads:
        load.wait()
    crossed = jnp.dot(attended, weights[...], preferred_element_type=F32)
    first = layer_norm(queries[...].astype(F32) + crossed, gain_ref[0:1]).astype(BF16)
    for i in range(out_ref.shape[0]):
        out_ref[i] = first


def first_state_of(parts, queries, proj, gain, copies):
    rows, width = parts[0].shape[0] - HEADS, parts[0].shape[1]
    local = pl.BlockSpec(memory_space=pltpu.VMEM)
    hbm = pl.BlockSpec(memory_space=pltpu.HBM)
    return pl.pallas_call(
        first_kernel,
        in_specs=[local] * 4 + [hbm, hbm, local],
        out_specs=local,
        scratch_shapes=[
            pltpu.VMEM((rows, width), BF16),
            pltpu.VMEM((width, width), BF16),
            pltpu.SemaphoreType.DMA((2,)),
        ],
        out_shape=jax.ShapeDtypeStruct((copies, rows, width), BF16),
        compiler_params=pltpu.CompilerParams(vmem_limit_bytes=SMALL),
        name="first_state",
    )(
        *parts,
        queries.reshape(copies, 2, rows, width),
        proj,
        gain,
    )


def stack_heads(array, rows):
    stacked = jnp.concatenate([array] * HEADS, axis=0)
    row_head = lax.broadcasted_iota(jnp.int32, stacked.shape, 0) // rows
    col_head = lax.broadcasted_iota(jnp.int32, stacked.shape, 1) // (stacked.shape[1] // HEADS)
    mine = row_head == col_head
    return jnp.where(mine, stacked, 0), mine


def near_kernel(
    first_ref,
    state_ref,
    pos_hbm,
    proj_hbm,
    absorbed_ref,
    mixed_ref,
    stat_ref,
    own_pos,
    pos,
    weights,
    sems,
):
    groups, rows, width = state_ref.shape
    core = lax.axis_index("c")
    loads = start_all(
        (
            (proj_hbm.at[pl.ds(0, 2)], weights),
            (pos_hbm.at[column(), core], own_pos),
            (pos_hbm.at[:, core], pos),
        ),
        sems,
    )
    for load in loads[:2]:
        load.wait()
    scale = math.log2(math.e) / math.sqrt(width // HEADS)
    self_in = first_ref[0] + own_pos[...]
    q_self = jnp.dot(self_in, weights[0], preferred_element_type=F32) * scale
    stacked, _ = stack_heads(q_self.astype(BF16), rows)
    absorbed = lax.dot_general(stacked, weights[1], NT, preferred_element_type=F32).astype(BF16)
    absorbed_ref[...] = absorbed
    state = state_ref[...].reshape(groups * rows, width)
    loads[2].wait()
    inputs = state + pos[...].reshape(groups * rows, width)
    scores = lax.dot_general(absorbed, inputs, NT, preferred_element_type=F32)
    peak = jnp.max(scores, axis=1, keepdims=True)
    weights_here = jnp.exp2(scores - peak)
    total = jnp.sum(weights_here, axis=1, keepdims=True)
    mixed_ref[...] = jnp.dot(weights_here.astype(BF16), state, preferred_element_type=F32)
    lane = lax.broadcasted_iota(jnp.int32, stat_ref.shape, 1)
    stat_ref[...] = jnp.where(lane == 0, peak, total)


def near_half(first, own, query_pos, proj):
    groups, rows, width = own.shape
    local = pl.BlockSpec(memory_space=pltpu.VMEM)
    hbm = pl.BlockSpec(memory_space=pltpu.HBM)
    shapes = [(HEADS * rows, width), (HEADS * rows, width), (HEADS * rows, LANES)]
    return pl.pallas_call(
        near_kernel,
        in_specs=[local, local, hbm, hbm],
        out_specs=[local] * 3,
        scratch_shapes=[
            pltpu.VMEM((rows, width), BF16),
            pltpu.VMEM(own.shape, BF16),
            pltpu.VMEM((2, width, width), BF16),
            pltpu.SemaphoreType.DMA((3,)),
        ],
        out_shape=[
            jax.ShapeDtypeStruct(shape, kind) for shape, kind in zip(shapes, (BF16, F32, F32))
        ],
        compiler_params=pltpu.CompilerParams(vmem_limit_bytes=SMALL),
        cost_estimate=pl.CostEstimate(
            flops=2**33, bytes_accessed=2**22, transcendentals=2**20
        ),
        name="near_half",
    )(first, own, query_pos.reshape(groups, 2, rows, width), proj)


def tail_kernel(
    first_ref,
    absorbed_ref,
    mixed_ref,
    stat_ref,
    state_ref,
    pos_hbm,
    proj_hbm,
    mlp_in_hbm,
    mlp_out_hbm,
    gain_ref,
    out_ref,
    pos,
    proj_ref,
    mlp_in_ref,
    mlp_out_ref,
    sems,
):
    loads = start_all(
        (
            (pos_hbm.at[:, 1 - lax.axis_index("c")], pos),
            (proj_hbm.at[pl.ds(2, 2)], proj_ref),
            (mlp_in_hbm, mlp_in_ref),
            (mlp_out_hbm, mlp_out_ref),
        ),
        sems,
    )
    _, rows, width = first_ref.shape
    keys = state_ref.shape[0] * state_ref.shape[1]
    state = state_ref[...].reshape(keys, width)
    loads[0].wait()
    inputs = state + pos[...].reshape(keys, width)
    scores = lax.dot_general(absorbed_ref[...], inputs, NT, preferred_element_type=F32)
    peak_a, total_a = stat_ref[:, 0:1], stat_ref[:, 1:2]
    peak_b = jnp.max(scores, axis=1, keepdims=True)
    peak = jnp.maximum(peak_a, peak_b)
    weights = jnp.exp2(scores - peak)
    factor = jnp.exp2(peak_a - peak)
    total = factor * total_a + jnp.sum(weights, axis=1, keepdims=True)
    mixed = factor * mixed_ref[...]
    mixed += jnp.dot(weights.astype(BF16), state, preferred_element_type=F32)
    mixed = (mixed / total).astype(BF16)
    loads[1].wait()
    blended = jnp.dot(mixed, proj_ref[0], preferred_element_type=F32)
    head_size = width // HEADS
    column = lax.broadcasted_iota(jnp.int32, (rows, width), 1) // head_size
    self_out = jnp.zeros((rows, width), F32)
    for head in range(HEADS):
        self_out = jnp.where(column == head, blended[head * rows : (head + 1) * rows], self_out)
    second = first_ref[0].astype(F32) + jnp.dot(
        self_out.astype(BF16), proj_ref[1], preferred_element_type=F32
    )
    second = layer_norm(second, gain_ref[1:2]).astype(BF16)
    loads[2].wait()
    hidden = jnp.dot(second, mlp_in_ref[...], preferred_element_type=F32)
    hidden = jnp.maximum(hidden, 0.0).astype(BF16)
    loads[3].wait()
    decoded = second.astype(F32) + jnp.dot(hidden, mlp_out_ref[...], preferred_element_type=F32)
    out_ref[...] = layer_norm(decoded, gain_ref[2:3]).astype(BF16)


def tail(first, partial, other, query_pos, proj, mlp_in, mlp_out, gain):
    groups, rows, width = other.shape
    local = pl.BlockSpec(memory_space=pltpu.VMEM)
    hbm = pl.BlockSpec(memory_space=pltpu.HBM)
    return pl.pallas_call(
        tail_kernel,
        in_specs=[local] * 5 + [hbm] * 4 + [local],
        out_specs=local,
        scratch_shapes=[
            pltpu.VMEM(other.shape, BF16),
            pltpu.VMEM((2, width, width), BF16),
            pltpu.VMEM(mlp_in.shape, BF16),
            pltpu.VMEM(mlp_out.shape, BF16),
            pltpu.SemaphoreType.DMA((4,)),
        ],
        out_shape=jax.ShapeDtypeStruct((rows, width), BF16),
        compiler_params=pltpu.CompilerParams(vmem_limit_bytes=SMALL),
        name="tail",
    )(
        first,
        *partial,
        other,
        query_pos.reshape(groups, 2, rows, width),
        proj,
        mlp_in,
        mlp_out,
        gain,
    )


def body(
    queries,
    query_pos,
    patches,
    patch_level,
    patch_sheet,
    query_sheets,
    level_embed,
    cross_proj,
    self_proj,
    mlp_in,
    mlp_out,
    norm_gain,
):
    square = lax.axis_size("x") * lax.axis_size("y")
    bands = lax.axis_size("z")
    swap = [(0, 1), (1, 0)]
    own = (patches, patch_level, patch_sheet)
    other = [lax.ppermute(array, "c", swap) for array in own]
    parts = cross_partial(queries, query_pos, query_sheets, own, other, level_embed, cross_proj)
    parts = lax.all_to_all(parts, ("x", "y"), 0, 0, tiled=True)
    part = merge(merge_kernel, parts.shape[1:], parts)
    part = merge(
        merge_two_kernel,
        part.shape,
        part,
        lax.ppermute(part, "z", [(i, i ^ 1) for i in range(bands)]),
    )
    sign = lambda i: 1 - 2 * (i % 2)
    shift = lambda hop: lax.ppermute(
        part, "z", [(i, (i + hop * sign(i)) % bands) for i in range(bands)]
    )
    near, middle, far = shift(-1), shift(-2), shift(-3)
    first = first_state_of(
        (part, far, near, middle),
        queries,
        cross_proj,
        norm_gain,
        square,
    )
    own = lax.all_to_all(first, ("x", "y"), 0, 0, tiled=True)
    other = lax.ppermute(own, "c", swap)
    partial = near_half(first, own, query_pos, self_proj)
    return tail(first, partial, other, query_pos, self_proj, mlp_in, mlp_out, norm_gain)


def solution(mesh):
    devices = mesh.devices
    names = ("z", "x", "y", "c")
    grid = Mesh(devices.reshape(devices.shape[0], 4, 4, 2), names)
    return jax.shard_map(
        body,
        mesh=grid,
        in_specs=(P(), P(), P(names, None), P(names), P(names)) + (P(),) * 7,
        out_specs=P(names[1:], None),
        check_vma=False,
    )
```

```python
import functools
import math

import jax
import jax.numpy as jnp
from jax import lax
from jax.experimental import pallas as pl
from jax.experimental.pallas import tpu as pltpu
from jax.sharding import Mesh
from jax.sharding import PartitionSpec as P

HEADS = 8
LANES = 128
NEG = -1e30
SMALL = 32 * 2**20
LARGE = 63_400_000
NT = (((1,), (1,)), ((), ()))
F32 = jnp.float32
BF16 = jnp.bfloat16


def layer_norm(values, gain):
    center = jnp.mean(values, axis=-1, keepdims=True)
    shifted = values - center
    spread = jnp.mean(shifted * shifted, axis=-1, keepdims=True)
    return shifted * lax.rsqrt(spread + 1e-05) * gain


def pieces(value):
    hi = value.astype(BF16).astype(F32)
    mid = (value - hi).astype(BF16).astype(F32)
    return hi, mid, value - hi - mid


def project_patches(patches, level_ids, sheet_ids, sheets, level_rows, w_key, w_value):
    rows, width = patches.shape
    row = lax.broadcasted_iota(jnp.int32, (LANES, rows), 0)
    held = (row == sheet_ids.reshape(1, rows)) | (row == level_ids.reshape(1, rows) + sheets)
    held = jnp.transpose(jnp.where(held, 1.0, 0.0)).astype(BF16)
    added = jnp.dot(held, level_rows, preferred_element_type=F32)
    key_input = (patches.astype(F32) + added).astype(BF16)
    keys = jnp.dot(key_input, w_key, preferred_element_type=F32).astype(BF16)
    values = jnp.dot(patches, w_value, preferred_element_type=F32).astype(BF16)
    return keys, values, held


def start_all(pairs, sems):
    loads = [
        pltpu.make_async_copy(source, target, sems.at[i]) for i, (source, target) in enumerate(pairs)
    ]
    for load in loads:
        load.start()
    return loads


def cross_kernel(
    level_a_hbm,
    sheet_a_hbm,
    level_b_hbm,
    sheet_b_hbm,
    level_hbm,
    sheets_hbm,
    patch_a_hbm,
    patch_b_hbm,
    queries_hbm,
    pos_hbm,
    proj_hbm,
    out_hbm,
    ids,
    level_ref,
    sheets_ref,
    out_ref,
    patches,
    queries,
    pos,
    proj,
    key_ref,
    value_ref,
    on_ref,
    sems,
    out_sems,
):
    core = lax.axis_index("c")
    groups, rows, width = queries.shape
    half = patch_a_hbm.shape[0]
    block = groups * rows
    head_size = width // HEADS
    loads = start_all(
        (
            (sheets_hbm, sheets_ref),
            (level_hbm, level_ref),
            (level_a_hbm, ids.at[0]),
            (sheet_a_hbm, ids.at[1]),
            (level_b_hbm, ids.at[2]),
            (sheet_b_hbm, ids.at[3]),
            (proj_hbm.at[pl.ds(1, 2)], proj.at[pl.ds(1, 2)]),
            (patch_a_hbm, patches.at[0]),
            (patch_b_hbm, patches.at[1]),
            (proj_hbm.at[0], proj.at[0]),
            (queries_hbm.at[:, core], queries),
            (pos_hbm.at[:, core], pos),
        ),
        sems,
    )
    loads[0].wait()
    sheets = sheets_ref.shape[0]
    cut = lax.broadcasted_iota(jnp.int32, (sheets, LANES), 1) < rows
    picked = []
    for start in range(0, 2 * block, 2 * LANES):
        even = sheets_ref[:, start : start + LANES]
        odd = sheets_ref[:, start + LANES : start + 2 * LANES]
        low = jnp.where(cut, even, pltpu.roll(odd, rows, 1))
        high = jnp.where(cut, pltpu.roll(even, rows, 1), odd)
        picked.append(jnp.where(core == 0, low, high))
    barred = jnp.where(jnp.concatenate(picked, axis=1) == 1, 0.0, NEG)
    barred = jnp.concatenate([barred, jnp.zeros((LANES - sheets, block), F32)], axis=0)
    barred = jnp.transpose(barred).astype(BF16)
    for load in loads[1:7]:
        load.wait()
    row = lax.broadcasted_iota(jnp.int32, (LANES, width), 0)
    level_rows = jnp.zeros((LANES, width), F32)
    for index in range(level_ref.shape[0]):
        added = level_ref[index : index + 1].astype(F32)
        level_rows = jnp.where(row == sheets + index, added, level_rows)
    level_rows = level_rows.astype(BF16)
    for i in range(2):
        loads[7 + i].wait()
        cut = pl.ds(i * half, half)
        key_ref[cut], value_ref[cut], on_ref[cut] = project_patches(
            patches[i], ids[2 * i], ids[2 * i + 1], sheets, level_rows, proj[1], proj[2]
        )
    for load in loads[9:]:
        load.wait()
    mixed = queries[...].reshape(block, width) + pos[...].reshape(block, width)
    scale = math.log2(math.e) / math.sqrt(head_size)
    q_all = (jnp.dot(mixed, proj[0], preferred_element_type=F32) * scale).astype(BF16)
    lane = lax.broadcasted_iota(jnp.int32, (block, LANES), 1)
    ones = jnp.ones((2 * half, LANES), BF16)
    peaks = jnp.zeros((block, LANES), F32)
    totals = jnp.zeros((block, LANES), F32)

    def score(head):
        cut = slice(head // 2 * LANES, head // 2 * LANES + LANES)
        inside = lane // head_size == head % 2
        left = jnp.concatenate([jnp.where(inside, q_all[:, cut], 0), barred], axis=1)
        right = jnp.concatenate([key_ref[:, cut], on_ref[...]], axis=1)
        return lax.dot_general(left, right, NT, preferred_element_type=F32)

    def store(cut):
        copy = pltpu.make_async_copy(
            out_ref.at[:, :, cut], out_hbm.at[:, :, cut], out_sems.at[cut.start // LANES]
        )
        copy.start()
        return copy

    scores = score(0)
    sums = None
    for head in range(HEADS):
        now, scores = scores, score(head + 1) if head + 1 < HEADS else None
        cut = slice(head // 2 * LANES, head // 2 * LANES + LANES)
        peak = jnp.max(now, axis=1, keepdims=True)
        weights = jnp.exp2(now - peak).astype(BF16)
        values = jnp.concatenate([value_ref[:, cut], ones], axis=1)
        part = jnp.dot(weights, values, preferred_element_type=F32)
        here = lane % HEADS == head
        peaks = jnp.where(here, peak, peaks)
        totals = jnp.where(here, part[:, LANES:], totals)
        if head % 2 == 0:
            sums = part[:, :LANES]
        else:
            sums = jnp.where(lane // head_size == 0, sums, part[:, :LANES])
            sums = sums.astype(BF16).reshape(groups, rows, LANES)
            for group in range(groups):
                out_ref[group, :rows, cut] = sums[group]
    kind = lane // HEADS
    hi, mid, low = pieces(peaks)
    stats = jnp.where(kind == 0, hi, jnp.where(kind == 1, mid, jnp.where(kind == 2, low, totals)))
    stats = jnp.transpose(stats)
    for group in range(0, groups, 2):
        cut = slice(group * rows, group * rows + LANES)
        tile = [stats[k * HEADS : k * HEADS + HEADS, cut] for k in range(width // LANES)]
        tile = jnp.concatenate(tile, axis=1).astype(BF16)
        out_ref[group, rows:] = tile
        out_ref[group + 1, rows:] = tile
    stores = [store(slice(i, i + LANES)) for i in range(0, width, LANES)]
    for copy in stores:
        copy.wait()


def cross_partial(queries, query_pos, query_sheets, own, other, level, proj):
    total, width = queries.shape
    rows = 64
    groups = total // (2 * rows)
    half = own[0].shape[0]
    view = lambda array: array.reshape(groups, 2, rows, array.shape[1])
    hbm = pl.BlockSpec(memory_space=pltpu.HBM)
    return pl.pallas_call(
        cross_kernel,
        in_specs=[hbm] * 11,
        out_specs=hbm,
        scratch_shapes=[
            pltpu.VMEM((4, half), jnp.int32),
            pltpu.VMEM(level.shape, BF16),
            pltpu.VMEM(query_sheets.shape[::-1], jnp.int32),
            pltpu.VMEM((groups, rows + HEADS, width), BF16),
            pltpu.VMEM((2, half, width), BF16),
            pltpu.VMEM((groups, rows, width), BF16),
            pltpu.VMEM((groups, rows, width), BF16),
            pltpu.VMEM((3, width, width), BF16),
            pltpu.VMEM((2 * half, width), BF16),
            pltpu.VMEM((2 * half, width), BF16),
            pltpu.VMEM((2 * half, LANES), BF16),
            pltpu.SemaphoreType.DMA((12,)),
            pltpu.SemaphoreType.DMA((width // LANES,)),
        ],
        out_shape=jax.ShapeDtypeStruct((groups, rows + HEADS, width), BF16),
        compiler_params=pltpu.CompilerParams(vmem_limit_bytes=LARGE),
        name="cross_partial",
    )(
        *own[1:],
        *other[1:],
        level,
        query_sheets.T,
        own[0],
        other[0],
        view(queries),
        view(query_pos),
        proj,
    )


def by_row(table, rows):
    if table.shape[0] < LANES:
        rest = jnp.zeros((LANES - table.shape[0], LANES), F32)
        table = jnp.concatenate([table, rest], axis=0)
    table = jnp.transpose(table)
    odd = lax.rem(column(), 2)
    return jnp.where(odd == 0, table[:rows], table[rows : 2 * rows])


def head_columns(width):
    shape = (LANES, width)
    head = lax.broadcasted_iota(jnp.int32, shape, 1) // (width // HEADS)
    same = lax.broadcasted_iota(jnp.int32, shape, 0) == head
    return jnp.where(same, 1.0, 0.0).astype(BF16)


def tree(terms):
    while len(terms) > 1:
        terms = [sum(terms[i : i + 2]) for i in range(0, len(terms), 2)]
    return terms[0]


def combine(refs):
    rows, width = refs[0].shape[0] - HEADS, refs[0].shape[1]
    stats = [ref[rows:].astype(F32) for ref in refs]
    cut = lambda s, k: s[:, k * LANES : k * LANES + LANES]
    peaks = [cut(s, 0) + cut(s, 1) + cut(s, 2) for s in stats]
    top = functools.reduce(jnp.maximum, peaks)
    factors = [jnp.exp2(peak - top).astype(BF16).astype(F32) for peak in peaks]
    total = tree([f * cut(s, 3) for f, s in zip(factors, stats)])
    table = by_row(jnp.concatenate(factors, axis=0), rows)
    spread = head_columns(width)
    sums = []
    for i, ref in enumerate(refs):
        factor = table if i == 0 else pltpu.roll(table, LANES - i * HEADS, 1)
        factor = jnp.dot(factor.astype(BF16), spread, preferred_element_type=F32)
        sums.append(factor * ref[:rows].astype(F32))
    return tree(sums), top, total


def write_merged(out_ref, sums, top, total):
    rows = sums.shape[0]
    out_ref[:rows] = sums.astype(BF16)
    out_ref[rows:] = jnp.concatenate([*pieces(top), total], axis=1).astype(BF16)


def merge_kernel(parts_ref, out_ref):
    write_merged(out_ref, *combine([parts_ref.at[i] for i in range(parts_ref.shape[0])]))


def merge_two_kernel(a_ref, b_ref, out_ref):
    write_merged(out_ref, *combine([a_ref, b_ref]))


def merge(kernel, shape, *operands):
    return pl.pallas_call(
        kernel,
        out_shape=jax.ShapeDtypeStruct(shape, BF16),
        compiler_params=pltpu.CompilerParams(vmem_limit_bytes=SMALL),
        name="merge",
    )(*operands)


def column():
    return lax.axis_index("x") * lax.axis_size("y") + lax.axis_index("y")


def first_kernel(
    a_ref,
    b_ref,
    c_ref,
    d_ref,
    queries_hbm,
    proj_hbm,
    gain_ref,
    out_ref,
    queries,
    weights,
    sems,
):
    loads = start_all(
        ((proj_hbm.at[3], weights), (queries_hbm.at[column(), lax.axis_index("c")], queries)), sems
    )
    sums, _, total = combine([a_ref, d_ref, b_ref, c_ref])
    rows, width = sums.shape
    spread = head_columns(width)
    total = tree(
        [
            jnp.dot(by_row(piece, rows).astype(BF16), spread, preferred_element_type=F32)
            for piece in pieces(total)
        ]
    )
    attended = (sums / total).astype(BF16)
    for load in loads:
        load.wait()
    crossed = jnp.dot(attended, weights[...], preferred_element_type=F32)
    first = layer_norm(queries[...].astype(F32) + crossed, gain_ref[0:1]).astype(BF16)
    for i in range(out_ref.shape[0]):
        out_ref[i] = first


def first_state_of(parts, queries, proj, gain, copies):
    rows, width = parts[0].shape[0] - HEADS, parts[0].shape[1]
    local = pl.BlockSpec(memory_space=pltpu.VMEM)
    hbm = pl.BlockSpec(memory_space=pltpu.HBM)
    return pl.pallas_call(
        first_kernel,
        in_specs=[local] * 4 + [hbm, hbm, local],
        out_specs=local,
        scratch_shapes=[
            pltpu.VMEM((rows, width), BF16),
            pltpu.VMEM((width, width), BF16),
            pltpu.SemaphoreType.DMA((2,)),
        ],
        out_shape=jax.ShapeDtypeStruct((copies, rows, width), BF16),
        compiler_params=pltpu.CompilerParams(vmem_limit_bytes=SMALL),
        name="first_state",
    )(
        *parts,
        queries.reshape(copies, 2, rows, width),
        proj,
        gain,
    )


def stack_heads(array, rows):
    stacked = jnp.concatenate([array] * HEADS, axis=0)
    row_head = lax.broadcasted_iota(jnp.int32, stacked.shape, 0) // rows
    col_head = lax.broadcasted_iota(jnp.int32, stacked.shape, 1) // (stacked.shape[1] // HEADS)
    mine = row_head == col_head
    return jnp.where(mine, stacked, 0), mine


def near_kernel(
    first_ref,
    state_ref,
    pos_hbm,
    proj_hbm,
    absorbed_ref,
    mixed_ref,
    stat_ref,
    own_pos,
    pos,
    weights,
    sems,
):
    groups, rows, width = state_ref.shape
    core = lax.axis_index("c")
    loads = start_all(
        (
            (proj_hbm.at[pl.ds(0, 2)], weights),
            (pos_hbm.at[column(), core], own_pos),
            (pos_hbm.at[:, core], pos),
        ),
        sems,
    )
    for load in loads[:2]:
        load.wait()
    scale = math.log2(math.e) / math.sqrt(width // HEADS)
    self_in = first_ref[0] + own_pos[...]
    q_self = jnp.dot(self_in, weights[0], preferred_element_type=F32) * scale
    stacked, _ = stack_heads(q_self.astype(BF16), rows)
    absorbed = lax.dot_general(stacked, weights[1], NT, preferred_element_type=F32).astype(BF16)
    absorbed_ref[...] = absorbed
    state = state_ref[...].reshape(groups * rows, width)
    loads[2].wait()
    inputs = state + pos[...].reshape(groups * rows, width)
    scores = lax.dot_general(absorbed, inputs, NT, preferred_element_type=F32)
    peak = jnp.max(scores, axis=1, keepdims=True)
    weights_here = jnp.exp2(scores - peak)
    total = jnp.sum(weights_here, axis=1, keepdims=True)
    mixed_ref[...] = jnp.dot(weights_here.astype(BF16), state, preferred_element_type=F32)
    lane = lax.broadcasted_iota(jnp.int32, stat_ref.shape, 1)
    stat_ref[...] = jnp.where(lane == 0, peak, total)


def near_half(first, own, query_pos, proj):
    groups, rows, width = own.shape
    local = pl.BlockSpec(memory_space=pltpu.VMEM)
    hbm = pl.BlockSpec(memory_space=pltpu.HBM)
    shapes = [(HEADS * rows, width), (HEADS * rows, width), (HEADS * rows, LANES)]
    return pl.pallas_call(
        near_kernel,
        in_specs=[local, local, hbm, hbm],
        out_specs=[local] * 3,
        scratch_shapes=[
            pltpu.VMEM((rows, width), BF16),
            pltpu.VMEM(own.shape, BF16),
            pltpu.VMEM((2, width, width), BF16),
            pltpu.SemaphoreType.DMA((3,)),
        ],
        out_shape=[
            jax.ShapeDtypeStruct(shape, kind) for shape, kind in zip(shapes, (BF16, F32, F32))
        ],
        compiler_params=pltpu.CompilerParams(vmem_limit_bytes=SMALL),
        cost_estimate=pl.CostEstimate(
            flops=2**33, bytes_accessed=2**22, transcendentals=2**20
        ),
        name="near_half",
    )(first, own, query_pos.reshape(groups, 2, rows, width), proj)


def tail_kernel(
    first_ref,
    absorbed_ref,
    mixed_ref,
    stat_ref,
    state_ref,
    pos_hbm,
    proj_hbm,
    mlp_in_hbm,
    mlp_out_hbm,
    gain_ref,
    out_ref,
    pos,
    proj_ref,
    mlp_in_ref,
    mlp_out_ref,
    sems,
):
    loads = start_all(
        (
            (pos_hbm.at[:, 1 - lax.axis_index("c")], pos),
            (proj_hbm.at[pl.ds(2, 2)], proj_ref),
            (mlp_in_hbm, mlp_in_ref),
            (mlp_out_hbm, mlp_out_ref),
        ),
        sems,
    )
    _, rows, width = first_ref.shape
    keys = state_ref.shape[0] * state_ref.shape[1]
    state = state_ref[...].reshape(keys, width)
    loads[0].wait()
    inputs = state + pos[...].reshape(keys, width)
    scores = lax.dot_general(absorbed_ref[...], inputs, NT, preferred_element_type=F32)
    peak_a, total_a = stat_ref[:, 0:1], stat_ref[:, 1:2]
    peak_b = jnp.max(scores, axis=1, keepdims=True)
    peak = jnp.maximum(peak_a, peak_b)
    weights = jnp.exp2(scores - peak)
    factor = jnp.exp2(peak_a - peak)
    total = factor * total_a + jnp.sum(weights, axis=1, keepdims=True)
    mixed = factor * mixed_ref[...]
    mixed += jnp.dot(weights.astype(BF16), state, preferred_element_type=F32)
    mixed = (mixed / total).astype(BF16)
    loads[1].wait()
    blended = jnp.dot(mixed, proj_ref[0], preferred_element_type=F32)
    head_size = width // HEADS
    column = lax.broadcasted_iota(jnp.int32, (rows, width), 1) // head_size
    self_out = jnp.zeros((rows, width), F32)
    for head in range(HEADS):
        self_out = jnp.where(column == head, blended[head * rows : (head + 1) * rows], self_out)
    second = first_ref[0].astype(F32) + jnp.dot(
        self_out.astype(BF16), proj_ref[1], preferred_element_type=F32
    )
    second = layer_norm(second, gain_ref[1:2]).astype(BF16)
    loads[2].wait()
    hidden = jnp.dot(second, mlp_in_ref[...], preferred_element_type=F32)
    hidden = jnp.maximum(hidden, 0.0).astype(BF16)
    loads[3].wait()
    decoded = second.astype(F32) + jnp.dot(hidden, mlp_out_ref[...], preferred_element_type=F32)
    out_ref[...] = layer_norm(decoded, gain_ref[2:3]).astype(BF16)


def tail(first, partial, other, query_pos, proj, mlp_in, mlp_out, gain):
    groups, rows, width = other.shape
    local = pl.BlockSpec(memory_space=pltpu.VMEM)
    hbm = pl.BlockSpec(memory_space=pltpu.HBM)
    return pl.pallas_call(
        tail_kernel,
        in_specs=[local] * 5 + [hbm] * 4 + [local],
        out_specs=local,
        scratch_shapes=[
            pltpu.VMEM(other.shape, BF16),
            pltpu.VMEM((2, width, width), BF16),
            pltpu.VMEM(mlp_in.shape, BF16),
            pltpu.VMEM(mlp_out.shape, BF16),
            pltpu.SemaphoreType.DMA((4,)),
        ],
        out_shape=jax.ShapeDtypeStruct((rows, width), BF16),
        compiler_params=pltpu.CompilerParams(vmem_limit_bytes=SMALL),
        name="tail",
    )(
        first,
        *partial,
        other,
        query_pos.reshape(groups, 2, rows, width),
        proj,
        mlp_in,
        mlp_out,
        gain,
    )


def body(
    queries,
    query_pos,
    patches,
    patch_level,
    patch_sheet,
    query_sheets,
    level_embed,
    cross_proj,
    self_proj,
    mlp_in,
    mlp_out,
    norm_gain,
):
    square = lax.axis_size("x") * lax.axis_size("y")
    bands = lax.axis_size("z")
    swap = [(0, 1), (1, 0)]
    own = (patches, patch_level, patch_sheet)
    other = [lax.ppermute(array, "c", swap) for array in own]
    parts = cross_partial(queries, query_pos, query_sheets, own, other, level_embed, cross_proj)
    parts = lax.all_to_all(parts, ("x", "y"), 0, 0, tiled=True)
    part = merge(merge_kernel, parts.shape[1:], parts)
    part = merge(
        merge_two_kernel,
        part.shape,
        part,
        lax.ppermute(part, "z", [(i, i ^ 1) for i in range(bands)]),
    )
    sign = lambda i: 1 - 2 * (i % 2)
    shift = lambda hop: lax.ppermute(
        part, "z", [(i, (i + hop * sign(i)) % bands) for i in range(bands)]
    )
    near, middle, far = shift(-1), shift(-2), shift(-3)
    first = first_state_of(
        (part, near, middle, far),
        queries,
        cross_proj,
        norm_gain,
        square,
    )
    own = lax.all_to_all(first, ("x", "y"), 0, 0, tiled=True)
    other = lax.ppermute(own, "c", swap)
    partial = near_half(first, own, query_pos, self_proj)
    return tail(first, partial, other, query_pos, self_proj, mlp_in, mlp_out, norm_gain)


def solution(mesh):
    devices = mesh.devices
    names = ("z", "x", "y", "c")
    grid = Mesh(devices.reshape(devices.shape[0], 4, 4, 2), names)
    return jax.shard_map(
        body,
        mesh=grid,
        in_specs=(P(), P(), P(names, None), P(names), P(names)) + (P(),) * 7,
        out_specs=P(names[1:], None),
        check_vma=False,
    )
```

```python
import functools
import math

import jax
import jax.numpy as jnp
from jax import lax
from jax.experimental import pallas as pl
from jax.experimental.pallas import tpu as pltpu
from jax.sharding import Mesh
from jax.sharding import PartitionSpec as P

HEADS = 8
LANES = 128
NEG = -1e30
SMALL = 32 * 2**20
LARGE = 63_400_000
NT = (((1,), (1,)), ((), ()))
F32 = jnp.float32
BF16 = jnp.bfloat16


def layer_norm(values, gain):
    center = jnp.mean(values, axis=-1, keepdims=True)
    shifted = values - center
    spread = jnp.mean(shifted * shifted, axis=-1, keepdims=True)
    return shifted * lax.rsqrt(spread + 1e-05) * gain


def pieces(value):
    hi = value.astype(BF16).astype(F32)
    mid = (value - hi).astype(BF16).astype(F32)
    return hi, mid, value - hi - mid


def project_patches(patches, level_ids, sheet_ids, sheets, level_rows, w_key, w_value):
    rows, width = patches.shape
    row = lax.broadcasted_iota(jnp.int32, (LANES, rows), 0)
    held = (row == sheet_ids.reshape(1, rows)) | (row == level_ids.reshape(1, rows) + sheets)
    held = jnp.transpose(jnp.where(held, 1.0, 0.0)).astype(BF16)
    added = jnp.dot(held, level_rows, preferred_element_type=F32)
    key_input = (patches.astype(F32) + added).astype(BF16)
    keys = jnp.dot(key_input, w_key, preferred_element_type=F32).astype(BF16)
    values = jnp.dot(patches, w_value, preferred_element_type=F32).astype(BF16)
    return keys, values, held


def start_all(pairs, sems):
    loads = [
        pltpu.make_async_copy(source, target, sems.at[i]) for i, (source, target) in enumerate(pairs)
    ]
    for load in loads:
        load.start()
    return loads


def cross_kernel(
    level_a_hbm,
    sheet_a_hbm,
    level_b_hbm,
    sheet_b_hbm,
    level_hbm,
    sheets_hbm,
    patch_a_hbm,
    patch_b_hbm,
    queries_hbm,
    pos_hbm,
    proj_hbm,
    out_hbm,
    ids,
    level_ref,
    sheets_ref,
    out_ref,
    patches,
    queries,
    pos,
    proj,
    key_ref,
    value_ref,
    on_ref,
    sems,
    out_sems,
):
    core = lax.axis_index("c")
    groups, rows, width = queries.shape
    half = patch_a_hbm.shape[0]
    block = groups * rows
    head_size = width // HEADS
    loads = start_all(
        (
            (sheets_hbm, sheets_ref),
            (level_hbm, level_ref),
            (level_a_hbm, ids.at[0]),
            (sheet_a_hbm, ids.at[1]),
            (level_b_hbm, ids.at[2]),
            (sheet_b_hbm, ids.at[3]),
            (proj_hbm.at[pl.ds(1, 2)], proj.at[pl.ds(1, 2)]),
            (patch_a_hbm, patches.at[0]),
            (patch_b_hbm, patches.at[1]),
            (proj_hbm.at[0], proj.at[0]),
            (queries_hbm.at[:, core], queries),
            (pos_hbm.at[:, core], pos),
        ),
        sems,
    )
    loads[0].wait()
    sheets = sheets_ref.shape[0]
    cut = lax.broadcasted_iota(jnp.int32, (sheets, LANES), 1) < rows
    picked = []
    for start in range(0, 2 * block, 2 * LANES):
        even = sheets_ref[:, start : start + LANES]
        odd = sheets_ref[:, start + LANES : start + 2 * LANES]
        low = jnp.where(cut, even, pltpu.roll(odd, rows, 1))
        high = jnp.where(cut, pltpu.roll(even, rows, 1), odd)
        picked.append(jnp.where(core == 0, low, high))
    barred = jnp.where(jnp.concatenate(picked, axis=1) == 1, 0.0, NEG)
    barred = jnp.concatenate([barred, jnp.zeros((LANES - sheets, block), F32)], axis=0)
    barred = jnp.transpose(barred).astype(BF16)
    for load in loads[1:7]:
        load.wait()
    row = lax.broadcasted_iota(jnp.int32, (LANES, width), 0)
    level_rows = jnp.zeros((LANES, width), F32)
    for index in range(level_ref.shape[0]):
        added = level_ref[index : index + 1].astype(F32)
        level_rows = jnp.where(row == sheets + index, added, level_rows)
    level_rows = level_rows.astype(BF16)
    for i in range(2):
        loads[7 + i].wait()
        cut = pl.ds(i * half, half)
        key_ref[cut], value_ref[cut], on_ref[cut] = project_patches(
            patches[i], ids[2 * i], ids[2 * i + 1], sheets, level_rows, proj[1], proj[2]
        )
    for load in loads[9:]:
        load.wait()
    mixed = queries[...].reshape(block, width) + pos[...].reshape(block, width)
    scale = math.log2(math.e) / math.sqrt(head_size)
    q_all = (jnp.dot(mixed, proj[0], preferred_element_type=F32) * scale).astype(BF16)
    lane = lax.broadcasted_iota(jnp.int32, (block, LANES), 1)
    ones = jnp.ones((2 * half, LANES), BF16)
    peaks = jnp.zeros((block, LANES), F32)
    totals = jnp.zeros((block, LANES), F32)

    def score(head):
        cut = slice(head // 2 * LANES, head // 2 * LANES + LANES)
        inside = lane // head_size == head % 2
        left = jnp.concatenate([jnp.where(inside, q_all[:, cut], 0), barred], axis=1)
        right = jnp.concatenate([key_ref[:, cut], on_ref[...]], axis=1)
        return lax.dot_general(left, right, NT, preferred_element_type=F32)

    def store(cut):
        copy = pltpu.make_async_copy(
            out_ref.at[:, :, cut], out_hbm.at[:, :, cut], out_sems.at[cut.start // LANES]
        )
        copy.start()
        return copy

    scores = score(0)
    sums = None
    for head in range(HEADS):
        now, scores = scores, score(head + 1) if head + 1 < HEADS else None
        cut = slice(head // 2 * LANES, head // 2 * LANES + LANES)
        peak = jnp.max(now, axis=1, keepdims=True)
        weights = jnp.exp2(now - peak).astype(BF16)
        values = jnp.concatenate([value_ref[:, cut], ones], axis=1)
        part = jnp.dot(weights, values, preferred_element_type=F32)
        here = lane % HEADS == head
        peaks = jnp.where(here, peak, peaks)
        totals = jnp.where(here, part[:, LANES:], totals)
        if head % 2 == 0:
            sums = part[:, :LANES]
        else:
            sums = jnp.where(lane // head_size == 0, sums, part[:, :LANES])
            sums = sums.astype(BF16).reshape(groups, rows, LANES)
            for group in range(groups):
                out_ref[group, :rows, cut] = sums[group]
    kind = lane // HEADS
    hi, mid, low = pieces(peaks)
    stats = jnp.where(kind == 0, hi, jnp.where(kind == 1, mid, jnp.where(kind == 2, low, totals)))
    stats = jnp.transpose(stats)
    for group in range(0, groups, 2):
        cut = slice(group * rows, group * rows + LANES)
        tile = [stats[k * HEADS : k * HEADS + HEADS, cut] for k in range(width // LANES)]
        tile = jnp.concatenate(tile, axis=1).astype(BF16)
        out_ref[group, rows:] = tile
        out_ref[group + 1, rows:] = tile
    stores = [store(slice(i, i + LANES)) for i in range(0, width, LANES)]
    for copy in stores:
        copy.wait()


def cross_partial(queries, query_pos, query_sheets, own, other, level, proj):
    total, width = queries.shape
    rows = 64
    groups = total // (2 * rows)
    half = own[0].shape[0]
    view = lambda array: array.reshape(groups, 2, rows, array.shape[1])
    hbm = pl.BlockSpec(memory_space=pltpu.HBM)
    return pl.pallas_call(
        cross_kernel,
        in_specs=[hbm] * 11,
        out_specs=hbm,
        scratch_shapes=[
            pltpu.VMEM((4, half), jnp.int32),
            pltpu.VMEM(level.shape, BF16),
            pltpu.VMEM(query_sheets.shape[::-1], jnp.int32),
            pltpu.VMEM((groups, rows + HEADS, width), BF16),
            pltpu.VMEM((2, half, width), BF16),
            pltpu.VMEM((groups, rows, width), BF16),
            pltpu.VMEM((groups, rows, width), BF16),
            pltpu.VMEM((3, width, width), BF16),
            pltpu.VMEM((2 * half, width), BF16),
            pltpu.VMEM((2 * half, width), BF16),
            pltpu.VMEM((2 * half, LANES), BF16),
            pltpu.SemaphoreType.DMA((12,)),
            pltpu.SemaphoreType.DMA((width // LANES,)),
        ],
        out_shape=jax.ShapeDtypeStruct((groups, rows + HEADS, width), BF16),
        compiler_params=pltpu.CompilerParams(vmem_limit_bytes=LARGE),
        name="cross_partial",
    )(
        *own[1:],
        *other[1:],
        level,
        query_sheets.T,
        own[0],
        other[0],
        view(queries),
        view(query_pos),
        proj,
    )


def by_row(table, rows):
    if table.shape[0] < LANES:
        rest = jnp.zeros((LANES - table.shape[0], LANES), F32)
        table = jnp.concatenate([table, rest], axis=0)
    table = jnp.transpose(table)
    odd = lax.rem(column(), 2)
    return jnp.where(odd == 0, table[:rows], table[rows : 2 * rows])


def head_columns(width):
    shape = (LANES, width)
    head = lax.broadcasted_iota(jnp.int32, shape, 1) // (width // HEADS)
    same = lax.broadcasted_iota(jnp.int32, shape, 0) == head
    return jnp.where(same, 1.0, 0.0).astype(BF16)


def tree(terms):
    while len(terms) > 1:
        terms = [sum(terms[i : i + 2]) for i in range(0, len(terms), 2)]
    return terms[0]


def combine(refs):
    rows, width = refs[0].shape[0] - HEADS, refs[0].shape[1]
    stats = [ref[rows:].astype(F32) for ref in refs]
    cut = lambda s, k: s[:, k * LANES : k * LANES + LANES]
    peaks = [cut(s, 0) + cut(s, 1) + cut(s, 2) for s in stats]
    top = functools.reduce(jnp.maximum, peaks)
    factors = [jnp.exp2(peak - top).astype(BF16).astype(F32) for peak in peaks]
    total = tree([f * cut(s, 3) for f, s in zip(factors, stats)])
    table = by_row(jnp.concatenate(factors, axis=0), rows)
    spread = head_columns(width)
    sums = []
    for i, ref in enumerate(refs):
        factor = table if i == 0 else pltpu.roll(table, LANES - i * HEADS, 1)
        factor = jnp.dot(factor.astype(BF16), spread, preferred_element_type=F32)
        sums.append(factor * ref[:rows].astype(F32))
    return tree(sums), top, total


def write_merged(out_ref, sums, top, total):
    rows = sums.shape[0]
    out_ref[:rows] = sums.astype(BF16)
    out_ref[rows:] = jnp.concatenate([*pieces(top), total], axis=1).astype(BF16)


def merge_kernel(parts_ref, out_ref):
    write_merged(out_ref, *combine([parts_ref.at[i] for i in range(parts_ref.shape[0])]))


def merge_two_kernel(a_ref, b_ref, out_ref):
    write_merged(out_ref, *combine([a_ref, b_ref]))


def merge(kernel, shape, *operands):
    return pl.pallas_call(
        kernel,
        out_shape=jax.ShapeDtypeStruct(shape, BF16),
        compiler_params=pltpu.CompilerParams(vmem_limit_bytes=SMALL),
        name="merge",
    )(*operands)


def column():
    return lax.axis_index("x") * lax.axis_size("y") + lax.axis_index("y")


def first_kernel(
    a_ref,
    b_ref,
    c_ref,
    d_ref,
    queries_hbm,
    proj_hbm,
    gain_ref,
    out_ref,
    queries,
    weights,
    sems,
):
    loads = start_all(
        ((proj_hbm.at[3], weights), (queries_hbm.at[column(), lax.axis_index("c")], queries)), sems
    )
    sums, _, total = combine([a_ref, d_ref, b_ref, c_ref])
    rows, width = sums.shape
    spread = head_columns(width)
    total = tree(
        [
            jnp.dot(by_row(piece, rows).astype(BF16), spread, preferred_element_type=F32)
            for piece in pieces(total)
        ]
    )
    attended = (sums / total).astype(BF16)
    for load in loads:
        load.wait()
    crossed = jnp.dot(attended, weights[...], preferred_element_type=F32)
    first = layer_norm(queries[...].astype(F32) + crossed, gain_ref[0:1]).astype(BF16)
    for i in range(out_ref.shape[0]):
        out_ref[i] = first


def first_state_of(parts, queries, proj, gain, copies):
    rows, width = parts[0].shape[0] - HEADS, parts[0].shape[1]
    local = pl.BlockSpec(memory_space=pltpu.VMEM)
    hbm = pl.BlockSpec(memory_space=pltpu.HBM)
    return pl.pallas_call(
        first_kernel,
        in_specs=[local] * 4 + [hbm, hbm, local],
        out_specs=local,
        scratch_shapes=[
            pltpu.VMEM((rows, width), BF16),
            pltpu.VMEM((width, width), BF16),
            pltpu.SemaphoreType.DMA((2,)),
        ],
        out_shape=jax.ShapeDtypeStruct((copies, rows, width), BF16),
        compiler_params=pltpu.CompilerParams(vmem_limit_bytes=SMALL),
        name="first_state",
    )(
        *parts,
        queries.reshape(copies, 2, rows, width),
        proj,
        gain,
    )


def stack_heads(array, rows):
    stacked = jnp.concatenate([array] * HEADS, axis=0)
    row_head = lax.broadcasted_iota(jnp.int32, stacked.shape, 0) // rows
    col_head = lax.broadcasted_iota(jnp.int32, stacked.shape, 1) // (stacked.shape[1] // HEADS)
    mine = row_head == col_head
    return jnp.where(mine, stacked, 0), mine


def near_kernel(
    first_ref,
    state_ref,
    pos_hbm,
    proj_hbm,
    absorbed_ref,
    mixed_ref,
    stat_ref,
    own_pos,
    pos,
    weights,
    sems,
):
    groups, rows, width = state_ref.shape
    core = lax.axis_index("c")
    loads = start_all(
        (
            (proj_hbm.at[pl.ds(0, 2)], weights),
            (pos_hbm.at[column(), core], own_pos),
            (pos_hbm.at[:, core], pos),
        ),
        sems,
    )
    for load in loads[:2]:
        load.wait()
    scale = math.log2(math.e) / math.sqrt(width // HEADS)
    self_in = first_ref[0] + own_pos[...]
    q_self = jnp.dot(self_in, weights[0], preferred_element_type=F32) * scale
    stacked, _ = stack_heads(q_self.astype(BF16), rows)
    absorbed = lax.dot_general(stacked, weights[1], NT, preferred_element_type=F32).astype(BF16)
    absorbed_ref[...] = absorbed
    state = state_ref[...].reshape(groups * rows, width)
    loads[2].wait()
    inputs = state + pos[...].reshape(groups * rows, width)
    scores = lax.dot_general(absorbed, inputs, NT, preferred_element_type=F32)
    peak = jnp.max(scores, axis=1, keepdims=True)
    weights_here = jnp.exp2(scores - peak)
    total = jnp.sum(weights_here, axis=1, keepdims=True)
    mixed_ref[...] = jnp.dot(weights_here.astype(BF16), state, preferred_element_type=F32)
    lane = lax.broadcasted_iota(jnp.int32, stat_ref.shape, 1)
    stat_ref[...] = jnp.where(lane == 0, peak, total)


def near_half(first, own, query_pos, proj):
    groups, rows, width = own.shape
    local = pl.BlockSpec(memory_space=pltpu.VMEM)
    hbm = pl.BlockSpec(memory_space=pltpu.HBM)
    shapes = [(HEADS * rows, width), (HEADS * rows, width), (HEADS * rows, LANES)]
    return pl.pallas_call(
        near_kernel,
        in_specs=[local, local, hbm, hbm],
        out_specs=[local] * 3,
        scratch_shapes=[
            pltpu.VMEM((rows, width), BF16),
            pltpu.VMEM(own.shape, BF16),
            pltpu.VMEM((2, width, width), BF16),
            pltpu.SemaphoreType.DMA((3,)),
        ],
        out_shape=[
            jax.ShapeDtypeStruct(shape, kind) for shape, kind in zip(shapes, (BF16, F32, F32))
        ],
        compiler_params=pltpu.CompilerParams(vmem_limit_bytes=SMALL),
        cost_estimate=pl.CostEstimate(
            flops=2**33, bytes_accessed=2**22, transcendentals=2**20
        ),
        name="near_half",
    )(first, own, query_pos.reshape(groups, 2, rows, width), proj)


def tail_kernel(
    first_ref,
    absorbed_ref,
    mixed_ref,
    stat_ref,
    state_ref,
    pos_hbm,
    proj_hbm,
    mlp_in_hbm,
    mlp_out_hbm,
    gain_ref,
    out_ref,
    pos,
    proj_ref,
    mlp_in_ref,
    mlp_out_ref,
    sems,
):
    loads = start_all(
        (
            (pos_hbm.at[:, 1 - lax.axis_index("c")], pos),
            (proj_hbm.at[pl.ds(2, 2)], proj_ref),
            (mlp_in_hbm, mlp_in_ref),
            (mlp_out_hbm, mlp_out_ref),
        ),
        sems,
    )
    _, rows, width = first_ref.shape
    keys = state_ref.shape[0] * state_ref.shape[1]
    state = state_ref[...].reshape(keys, width)
    loads[0].wait()
    inputs = state + pos[...].reshape(keys, width)
    scores = lax.dot_general(absorbed_ref[...], inputs, NT, preferred_element_type=F32)
    peak_a, total_a = stat_ref[:, 0:1], stat_ref[:, 1:2]
    peak_b = jnp.max(scores, axis=1, keepdims=True)
    peak = jnp.maximum(peak_a, peak_b)
    weights = jnp.exp2(scores - peak)
    factor = jnp.exp2(peak_a - peak)
    total = factor * total_a + jnp.sum(weights, axis=1, keepdims=True)
    mixed = factor * mixed_ref[...]
    mixed += jnp.dot(weights.astype(BF16), state, preferred_element_type=F32)
    mixed = (mixed / total).astype(BF16)
    loads[1].wait()
    blended = jnp.dot(mixed, proj_ref[0], preferred_element_type=F32)
    head_size = width // HEADS
    column = lax.broadcasted_iota(jnp.int32, (rows, width), 1) // head_size
    self_out = jnp.zeros((rows, width), F32)
    for head in range(HEADS):
        self_out = jnp.where(column == head, blended[head * rows : (head + 1) * rows], self_out)
    second = first_ref[0].astype(F32) + jnp.dot(
        self_out.astype(BF16), proj_ref[1], preferred_element_type=F32
    )
    second = layer_norm(second, gain_ref[1:2]).astype(BF16)
    loads[2].wait()
    hidden = jnp.dot(second, mlp_in_ref[...], preferred_element_type=F32)
    hidden = jnp.maximum(hidden, 0.0).astype(BF16)
    loads[3].wait()
    decoded = second.astype(F32) + jnp.dot(hidden, mlp_out_ref[...], preferred_element_type=F32)
    out_ref[...] = layer_norm(decoded, gain_ref[2:3]).astype(BF16)


def tail(first, partial, other, query_pos, proj, mlp_in, mlp_out, gain):
    groups, rows, width = other.shape
    local = pl.BlockSpec(memory_space=pltpu.VMEM)
    hbm = pl.BlockSpec(memory_space=pltpu.HBM)
    return pl.pallas_call(
        tail_kernel,
        in_specs=[local] * 5 + [hbm] * 4 + [local],
        out_specs=local,
        scratch_shapes=[
            pltpu.VMEM(other.shape, BF16),
            pltpu.VMEM((2, width, width), BF16),
            pltpu.VMEM(mlp_in.shape, BF16),
            pltpu.VMEM(mlp_out.shape, BF16),
            pltpu.SemaphoreType.DMA((4,)),
        ],
        out_shape=jax.ShapeDtypeStruct((rows, width), BF16),
        compiler_params=pltpu.CompilerParams(vmem_limit_bytes=SMALL),
        name="tail",
    )(
        first,
        *partial,
        other,
        query_pos.reshape(groups, 2, rows, width),
        proj,
        mlp_in,
        mlp_out,
        gain,
    )


def body(
    queries,
    query_pos,
    patches,
    patch_level,
    patch_sheet,
    query_sheets,
    level_embed,
    cross_proj,
    self_proj,
    mlp_in,
    mlp_out,
    norm_gain,
):
    square = lax.axis_size("x") * lax.axis_size("y")
    bands = lax.axis_size("z")
    swap = [(0, 1), (1, 0)]
    own = (patches, patch_level, patch_sheet)
    other = [lax.ppermute(array, "c", swap) for array in own]
    parts = cross_partial(queries, query_pos, query_sheets, own, other, level_embed, cross_proj)
    parts = lax.all_to_all(parts, ("x", "y"), 0, 0, tiled=True)
    part = merge(merge_kernel, parts.shape[1:], parts)
    part = merge(
        merge_two_kernel,
        part.shape,
        part,
        lax.ppermute(part, "z", [(i, i ^ 1) for i in range(bands)]),
    )
    sign = lambda i: 1 - 2 * (i % 2)
    shift = lambda hop: lax.ppermute(
        part, "z", [(i, (i + hop * sign(i)) % bands) for i in range(bands)]
    )
    near, middle, far = shift(-1), shift(-2), shift(-3)
    first = first_state_of(
        (part, middle, near, far),
        queries,
        cross_proj,
        norm_gain,
        square,
    )
    own = lax.all_to_all(first, ("x", "y"), 0, 0, tiled=True)
    other = lax.ppermute(own, "c", swap)
    partial = near_half(first, own, query_pos, self_proj)
    return tail(first, partial, other, query_pos, self_proj, mlp_in, mlp_out, norm_gain)


def solution(mesh):
    devices = mesh.devices
    names = ("z", "x", "y", "c")
    grid = Mesh(devices.reshape(devices.shape[0], 4, 4, 2), names)
    return jax.shard_map(
        body,
        mesh=grid,
        in_specs=(P(), P(), P(names, None), P(names), P(names)) + (P(),) * 7,
        out_specs=P(names[1:], None),
        check_vma=False,
    )
```
